256 devices in a mesh: seq: 8 (over y_lo, x), pos: 32 (over z, y_hi, core).
Axes of the slice: x: 4, y: 4 (y_hi: 2, y_lo: 2; y = y_hi * 2 + y_lo), z: 8, core: 2. Of those that a mesh axis runs over, the one named last changes fastest.
Arguments:
- y_rows: bfloat16 [64, 512, 3072], P('seq', 'pos'), may hold values from -6 to 6
- grad_res: bfloat16 [64, 512, 3072], P('seq', 'pos'), may hold values from -6 to 6
- shift: float32 [3072], replicated, may hold values from -3 to 3
- scale_mod: float32 [3072], replicated, may hold values from -0.5 to 0.5
- temporal_qkv: bfloat16 [3, 16, 64, 512, 128], P(None, 'seq', None, 'pos'), may hold values from -6 to 6
- temporal_grad: bfloat16 [16, 64, 512, 128], P('seq', None, 'pos'), may hold values from -6 to 6
- spatial_qkv: bfloat16 [3, 16, 64, 512, 128], P(None, 'seq', 'pos'), may hold values from -6 to 6
- spatial_out: bfloat16 [16, 64, 512, 128], P('seq', None, 'pos'), may hold values from -6 to 6
- w_temporal: bfloat16 [16, 3072, 3, 128], P('seq', 'pos'), may hold values from -0.109375 to 0.109375
- w_spatial: bfloat16 [16, 3072, 128], P('seq', 'pos'), may hold values from -0.125 to 0.125
Outputs:
- spatial_grads: bfloat16 [3, 16, 64, 512, 128], P(None, 'seq', None, 'pos')
- input_grad: bfloat16 [64, 512, 3072], P('seq', 'pos')
- w_temporal_grad: float32 [16, 3072, 3, 128], P('seq', 'pos')
- w_spatial_grad: float32 [16, 3072, 128], P('seq', 'pos')
The draws below stay inside these ranges and needn't reach their ends.
All inputs are finite; a program needn't handle non-finite values.
Results may differ from the reference program's by a relative error of at most 0.03.
Values may be sent and summed in bfloat16 or wider, within the bound.
A program may use at most 128 MiB of HBM per device.

```python
import jax
import jax.numpy as jnp
from jax import lax

D = 3072
HEADS = 16
HEAD_DIM = 128
POS_DEV = 16
FRAMES = 64
POSITIONS = 512
N_SEQ = 8
N_POS = 32


def draw_temporal_qkv(key, part):
    key = jax.random.fold_in(key, 17)
    shape = (3, HEADS, FRAMES, POSITIONS, HEAD_DIM)
    return jax.random.truncated_normal(key, -6.0, 6.0, shape, jnp.float32).astype(jnp.bfloat16)


def draw_spatial_qkv(key, part):
    key = jax.random.fold_in(key, 29)
    shape = (3, HEADS, FRAMES, POSITIONS, HEAD_DIM)
    return jax.random.truncated_normal(key, -6.0, 6.0, shape, jnp.float32).astype(jnp.bfloat16)


def with_spikes(array, key, source, target, blocks, factor):
    def block_of(axis_at):
        return (jnp.arange(array.shape[axis_at]) // (array.shape[axis_at] // blocks)).reshape((-1,) + (1,) * (array.ndim - 1 - axis_at))

    one_side = jax.random.permutation(key, blocks)[block_of(target)]
    other_side = (block_of(target) + blocks // 2) % blocks
    return jnp.where((block_of(source) == one_side) | (block_of(source) == other_side), factor * array, array)


def shard_levels(own_key, dims, cuts, smallest, high):
    loudness, own = 1.0, jax.random.fold_in(own_key, 6)
    for dim, shards_of in cuts:
        steps = jnp.exp(jax.random.uniform(jax.random.fold_in(own, dim), (shards_of,), jnp.float32, smallest / len(cuts), high / len(cuts)))
        loudness = loudness * jnp.repeat(steps, dims[dim] // shards_of).reshape([-1 if axis == dim else 1 for axis in range(len(dims))])
    return loudness


def gaussian(rng, dims, spread, limit, shards=(), kind=jnp.bfloat16):
    entries = jax.random.normal(rng, dims, jnp.float32) * spread
    if len(shards) > 0:
        entries = shard_levels(rng, dims, shards, -0.22, 0.18) * entries
    return jnp.clip(entries, min=-limit, max=limit).astype(kind)


def noise_with(key, extent, deviation, limit, cuts, heavy, kind=jnp.bfloat16):
    drawn = deviation * jax.random.normal(key, extent, jnp.float32)
    if cuts:
        drawn = drawn * shard_levels(key, extent, cuts, -0.22, 0.18)
    return jnp.clip(with_spikes(drawn, jax.random.fold_in(key, 3), *heavy), -limit, limit).astype(kind)


def setup_inputs(seed: int = 0) -> dict:
    streams_of = jax.random.split(jax.random.key(seed), 11)
    return {
        "y_rows": noise_with(streams_of[0], (FRAMES, POSITIONS, D), 1.0, 6.0, ((0, 8), (1, 32)), (1, 2, 32, 2.75)),
        "grad_res": gaussian(streams_of[1], (FRAMES, POSITIONS, D), 1.0, 6.0, ((0, 8), (1, 32))),
        "shift": gaussian(streams_of[2], (D,), 0.5, 3.0, (), jnp.float32),
        "scale_mod": jnp.clip(jax.random.uniform(streams_of[3], (D,), jnp.float32, -0.5, 0.5), -0.5, 0.5),
        "temporal_qkv": draw_temporal_qkv(jax.random.fold_in(streams_of[10], 71), 0),
        "temporal_grad": noise_with(streams_of[5], (HEADS, FRAMES, POSITIONS, HEAD_DIM), 1.0, 6.0, ((0, 8), (2, 32)), (0, 1, 8, 2.0)),
        "spatial_qkv": draw_spatial_qkv(jax.random.fold_in(streams_of[10], 71), 0),
        "spatial_out": gaussian(streams_of[7], (HEADS, FRAMES, POSITIONS, HEAD_DIM), 1.0, 6.0, ((0, 8), (2, 32))),
        "w_temporal": gaussian(streams_of[8], (HEADS, D, 3, HEAD_DIM), D ** -0.5, 0.109375, ((0, 8), (1, 32))),
        "w_spatial": gaussian(streams_of[9], (HEADS, D, HEAD_DIM), (HEADS * HEAD_DIM) ** -0.5, 0.125, ((0, 8), (1, 32))),
    }


def normalize(rows, shift, scale_mod):
    values = rows.astype(jnp.float32)
    center = values - lax.optimization_barrier(jnp.mean(values, axis=-1, keepdims=True))
    inverse = lax.rsqrt(lax.optimization_barrier(jnp.mean(center * center, axis=-1, keepdims=True)) + 1e-06)
    unit_rows = center * inverse
    normed = (unit_rows * (1.0 + scale_mod) + shift).astype(jnp.bfloat16)
    return (normed, unit_rows, inverse)

def norm_back(grad_normed, unit_rows, inverse, scale_mod):
    scaled = grad_normed * (1.0 + scale_mod)
    first_mean = lax.optimization_barrier(jnp.mean(scaled, axis=-1, keepdims=True))
    second_mean = lax.optimization_barrier(jnp.mean(scaled * unit_rows, axis=-1, keepdims=True))
    return inverse * (scaled - first_mean - unit_rows * second_mean)

def rounded(values):
    return lax.optimization_barrier(values.astype(jnp.bfloat16)).astype(jnp.float32)

def attention_back(queries, key_rows, value_rows, grad_out):
    factor = queries.shape[-1] ** (-0.5)
    scores = jnp.einsum('...ie,...je->...ij', queries, key_rows) * factor
    highest = lax.optimization_barrier(jnp.max(scores, axis=-1, keepdims=True))
    exponent = jnp.exp(scores - highest)
    attend = exponent / lax.optimization_barrier(jnp.sum(exponent, axis=-1, keepdims=True))
    attend_low = rounded(attend)
    grad_values = jnp.einsum('...ij,...ie->...je', attend_low, grad_out)
    grad_attend = jnp.einsum('...ie,...je->...ij', grad_out, value_rows)
    inner = lax.optimization_barrier(jnp.sum(attend * grad_attend, axis=-1, keepdims=True))
    grad_scores = rounded(attend * (grad_attend - inner) * factor)
    grad_queries = jnp.einsum('...ij,...je->...ie', grad_scores, key_rows)
    grad_keys = jnp.einsum('...ij,...ie->...je', grad_scores, queries)
    return jnp.stack([grad_queries, grad_keys, grad_values]).astype(jnp.bfloat16)

def temporal_head(inputs):
    head_qkv, head_grad = inputs
    swapped = jnp.swapaxes(head_qkv.astype(jnp.float32), 1, 2)
    cotangent = jnp.swapaxes(head_grad.astype(jnp.float32), 0, 1)
    result = attention_back(swapped[0], swapped[1], swapped[2], cotangent)
    return jnp.swapaxes(result, 1, 2)

def spatial_head(inputs):
    head_qkv, head_grad = inputs
    upcast = head_qkv.astype(jnp.float32)
    return attention_back(upcast[0], upcast[1], upcast[2], head_grad.astype(jnp.float32))

def reference(y_rows, grad_res, shift, scale_mod, temporal_qkv, temporal_grad, spatial_qkv, spatial_out, w_temporal, w_spatial):
    normed, unit_rows, inverse = normalize(y_rows, shift, scale_mod)
    grads_t = lax.map(temporal_head, (jnp.moveaxis(temporal_qkv, 1, 0), temporal_grad))
    grads_t = jnp.moveaxis(grads_t, 0, 1)
    group = HEADS // N_SEQ

    def head_group(total, index):
        part_grads = lax.dynamic_slice_in_dim(grads_t, index * group, group, 1).astype(jnp.float32)
        part_weights = lax.dynamic_slice_in_dim(w_temporal, index * group, group, 0).astype(jnp.float32)
        term = jnp.einsum('chfpe,hdce->fpd', part_grads, part_weights)
        return (total + rounded(term), None)
    start_total = jnp.zeros((FRAMES, POSITIONS, D), jnp.float32)
    grad_normed, _ = lax.scan(head_group, start_total, jnp.arange(N_SEQ, dtype=jnp.int32))
    grad_input = grad_res.astype(jnp.float32) + norm_back(grad_normed, unit_rows, inverse, scale_mod)
    input_grad = grad_input.astype(jnp.bfloat16)
    grad_spatial_out = jnp.einsum('fpd,hde->hfpe', input_grad.astype(jnp.float32), w_spatial.astype(jnp.float32)).astype(jnp.bfloat16)
    spatial_grads = lax.map(spatial_head, (jnp.moveaxis(spatial_qkv, 1, 0), grad_spatial_out))
    spatial_grads = jnp.moveaxis(spatial_grads, 0, 1)

    def position_block(totals, index):
        start = index * POS_DEV
        block_rows = lax.dynamic_slice_in_dim(normed, start, POS_DEV, 1).astype(jnp.float32)
        block_grads = lax.dynamic_slice_in_dim(grads_t, start, POS_DEV, 3).astype(jnp.float32)
        block_out = lax.dynamic_slice_in_dim(spatial_out, start, POS_DEV, 2).astype(jnp.float32)
        block_input = lax.dynamic_slice_in_dim(input_grad, start, POS_DEV, 1).astype(jnp.float32)
        temporal_term = jnp.einsum('fpd,chfpe->hdce', block_rows, block_grads)
        spatial_term = jnp.einsum('hfpe,fpd->hde', block_out, block_input)
        return ((totals[0] + rounded(temporal_term), totals[1] + rounded(spatial_term)), None)
    start_grads = (jnp.zeros((HEADS, D, 3, HEAD_DIM), jnp.float32), jnp.zeros((HEADS, D, HEAD_DIM), jnp.float32))
    weight_grads, _ = lax.scan(position_block, start_grads, jnp.arange(N_POS, dtype=jnp.int32))
    return (spatial_grads, input_grad, weight_grads[0], weight_grads[1])
```

```python
import functools

import jax
import jax.numpy as jnp
from jax import lax
from jax.experimental import pallas as pl
from jax.experimental.pallas import tpu as pltpu
from jax.sharding import PartitionSpec as P

MESH = pl.DeviceIdType.MESH
F32 = jnp.float32
BF16 = jnp.bfloat16
NT = (((1,), (1,)), ((), ()))
TN = (((0,), (0,)), ((), ()))
NN = (((1,), (0,)), ((), ()))


def dot(a, b, dims=NN):
    return lax.dot_general(a, b, dims, preferred_element_type=F32)


class Place:
    def __init__(self):
        s, p = lax.axis_index("seq"), lax.axis_index("pos")
        self.yl, self.x = s // 4, s % 4
        self.z, self.yh, self.co = p // 4, (p // 2) % 2, p % 2

    def at(self, yl=None, x=None, z=None, yh=None, co=None):
        yl = self.yl if yl is None else yl
        x = self.x if x is None else x
        z = self.z if z is None else z
        yh = self.yh if yh is None else yh
        co = self.co if co is None else co
        return (yl * 4 + x, z * 4 + yh * 2 + co)

    def dx(self, k):
        return (self.x + k + 4) % 4

    def dz(self, k):
        return (self.z + k + 8) % 8

    def neighbours(self, seq, pos):
        found = []
        if seq:
            found += [self.at(x=self.dx(1)), self.at(x=self.dx(-1)), self.at(yl=1 - self.yl)]
        if pos:
            found += [
                self.at(z=self.dz(1)),
                self.at(z=self.dz(-1)),
                self.at(yh=1 - self.yh),
                self.at(co=1 - self.co),
            ]
        return found


def meet(devices):
    barrier = pltpu.get_barrier_semaphore()
    for device in devices:
        pl.semaphore_signal(barrier, inc=1, device_id=device, device_id_type=MESH)
    pl.semaphore_wait(barrier, len(devices))


class Net:
    def __init__(self, send_sem, recv_sem):
        self.send_sem, self.recv_sem, self.count, self.open = send_sem, recv_sem, 0, []

    def send(self, source, target, device):
        i = self.count
        self.count += 1
        copy = pltpu.make_async_remote_copy(
            src_ref=source,
            dst_ref=target,
            send_sem=self.send_sem.at[i],
            recv_sem=self.recv_sem.at[i],
            device_id=device,
            device_id_type=MESH,
        )
        copy.start()
        self.open.append(copy)
        return copy

    def finish(self):
        for copy in self.open:
            copy.wait_send()
        self.open = []


def run_all(steps):
    live = list(steps)
    while live:
        for step in list(live):
            try:
                next(step)
            except StopIteration:
                live.remove(step)


def add_into(target, terms, rows, tile=16):
    def body(i, carry):
        at = pl.ds(pl.multiple_of(i * tile, tile), tile)
        total = target[at, :].astype(F32)
        for term in terms:
            total += term[at, :].astype(F32)
        target[at, :] = total.astype(BF16)
        return carry

    lax.fori_loop(0, rows // tile, body, 0)


def gather_pos(net, me, own, full):
    def slot(z, r, co):
        return full.at[z * 4 + ((me.yh + r) % 2) * 2 + co]

    up, down = me.at(z=me.dz(1)), me.at(z=me.dz(-1))
    other = me.at(co=1 - me.co)
    mine = slot(me.z, 0, me.co)
    cross = net.send(own, mine, me.at(yh=1 - me.yh))
    plus = [net.send(own, mine, up)]
    minus = [net.send(own, mine, down)]
    cores = [net.send(own, mine, other)]
    mine[...] = own[...]
    yield
    cross.wait_recv()
    near = slot(me.z, 1, me.co)
    plus.append(net.send(near, near, up))
    minus.append(net.send(near, near, down))
    cores.append(net.send(near, near, other))
    yield
    for k in range(1, 5):
        next_plus, next_minus = [], []
        for r in range(2):
            if k < 4 or r == 0:
                plus[r].wait_recv()
                block = slot(me.dz(-k), r, me.co)
                if k < 3 or (k == 3 and r == 0):
                    next_plus.append(net.send(block, block, up))
                else:
                    next_plus.append(None)
                cores.append(net.send(block, block, other))
            if k < 4 or r == 1:
                minus[r].wait_recv()
                block = slot(me.dz(k), r, me.co)
                if k < 3 or (k == 3 and r == 1):
                    next_minus.append(net.send(block, block, down))
                else:
                    next_minus.append(None)
                cores.append(net.send(block, block, other))
        plus, minus = next_plus, next_minus
        yield
    for copy in cores:
        copy.wait_recv()


def gather_seq(net, me, full, done):
    def part(yl, x, first, rows):
        return full.at[yl * 4 + x, pl.ds(first, rows), :]

    yl, x, far = me.yl, me.x, 1 - me.yl
    left, right, xo = me.dx(-1), me.dx(1), me.dx(2)
    to_r, to_l, to_y = me.at(x=right), me.at(x=left), me.at(yl=far)

    def push(block, device):
        return net.send(block, block, device)

    h0, h1 = part(yl, x, 0, 64), part(yl, x, 64, 64)
    y0 = push(h0, to_y)
    r0, l0 = push(h0, to_r), push(h0, to_l)
    y1 = push(h1, to_y)
    r1, l1 = push(h1, to_r), push(h1, to_l)
    done((yl, x))
    yield
    y0.wait_recv()
    f0 = part(far, x, 0, 64)
    rf, lf = push(f0, to_r), push(f0, to_l)
    r0.wait_recv()
    l0.wait_recv()
    ra = push(part(yl, left, 0, 32), to_r)
    lb = push(part(yl, right, 32, 32), to_l)
    y1.wait_recv()
    done((far, x))
    yield
    r1.wait_recv()
    l1.wait_recv()
    rc = push(part(yl, left, 64, 32), to_r)
    ld = push(part(yl, right, 96, 32), to_l)
    yr = push(part(yl, left, 64, 64), to_y)
    yq = push(part(yl, right, 64, 64), to_y)
    done((yl, left))
    done((yl, right))
    yield
    rf.wait_recv()
    lf.wait_recv()
    re = push(part(far, left, 0, 32), to_r)
    lg = push(part(far, right, 32, 32), to_l)
    ra.wait_recv()
    lb.wait_recv()
    yield
    rc.wait_recv()
    ld.wait_recv()
    yo = push(part(yl, xo, 64, 64), to_y)
    done((yl, xo))
    yield
    yr.wait_recv()
    yq.wait_recv()
    done((far, left))
    done((far, right))
    yield
    re.wait_recv()
    lg.wait_recv()
    yo.wait_recv()
    done((far, xo))


def reduce_x(net, me, block, quarter, half, started, result):
    left, right, xo = me.dx(-1), me.dx(1), me.dx(2)
    to_r, to_l = me.at(x=right), me.at(x=left)
    a = net.send(block(xo).at[pl.ds(0, 32)], quarter.at[0], to_r)
    b = net.send(block(xo).at[pl.ds(32, 32)], quarter.at[1], to_l)
    started()
    yield
    a.wait_recv()
    add_into(block(right).at[pl.ds(0, 32)], [quarter.at[0]], 32)
    c = net.send(block(right), half.at[0], to_r)
    b.wait_recv()
    add_into(block(left).at[pl.ds(32, 32)], [quarter.at[1]], 32)
    d = net.send(block(left), half.at[1], to_l)
    yield
    c.wait_recv()
    d.wait_recv()
    result()


def reduce_pos_ring(net, me, part, core_recv, core_copies, ring, across, out):
    up, down = me.at(z=me.dz(1)), me.at(z=me.dz(-1))

    def slot(z, r):
        return part.at[z, ((me.yh + r) % 2) * 2 + me.co]

    def merge(z, k):
        core_copies[k].wait_recv()
        for r in range(2):
            add_into(slot(z, r), [core_recv.at[z, (me.yh + r) % 2]], 96)

    merge(me.dz(4), 0)
    plus = [net.send(slot(me.dz(4), 0), ring.at[0, 0, 0], up), None]
    minus = [None, net.send(slot(me.dz(4), 1), ring.at[1, 0, 1], down)]
    merge(me.dz(3), 1)
    merge(me.dz(-3), 2)
    yield
    for k in range(1, 4):
        next_plus, next_minus = [], []
        for r in range(2):
            at = slot(me.dz(4 - k), r)
            if plus[r] is not None:
                plus[r].wait_recv()
                add_into(at, [ring.at[0, k - 1, r]], 96)
            next_plus.append(net.send(at, ring.at[0, k, r], up))
            at = slot(me.dz(k - 4), r)
            if minus[r] is not None:
                minus[r].wait_recv()
                add_into(at, [ring.at[1, k - 1, r]], 96)
            next_minus.append(net.send(at, ring.at[1, k, r], down))
        plus, minus = next_plus, next_minus
        if k < 3:
            merge(me.dz(3 - k), 2 * k + 1)
            merge(me.dz(k - 3), 2 * k + 2)
        else:
            merge(me.z, 7)
        yield
    for r in (1, 0):
        plus[r].wait_recv()
        minus[r].wait_recv()
        add_into(slot(me.z, r), [ring.at[0, 3, r], ring.at[1, 3, r]], 96)
        if r == 1:
            swap = net.send(slot(me.z, 1), across, me.at(yh=1 - me.yh))
    yield
    swap.wait_recv()
    out[...] = slot(me.z, 0)[...].astype(F32) + across[...].astype(F32)


def z_order(i):
    return 4 + (1 - 2 * (i % 2)) * ((i + 1) // 2)


def core_copy(me, part, core_recv, send_sem, recv_sem, zt, i):
    copies = []
    for yh in range(2):
        copies.append(
            pltpu.make_async_remote_copy(
                src_ref=part.at[zt, yh * 2 + 1 - me.co],
                dst_ref=core_recv.at[zt, yh],
                send_sem=send_sem.at[i, yh],
                recv_sem=recv_sem.at[i, yh],
                device_id=me.at(co=1 - me.co),
                device_id_type=MESH,
            )
        )
    return copies


class Pair:
    def __init__(self, copies):
        self.copies = copies

    def wait_recv(self):
        for copy in self.copies:
            copy.wait_recv()


def core_copies_of(me, part, core_recv, send_sem, recv_sem):
    return [
        Pair(core_copy(me, part, core_recv, send_sem, recv_sem, me.dz(z_order(i) - 8), i))
        for i in range(8)
    ]


def weight_partial(me, rows_ref, right, part, core_recv, send_sem, recv_sem):
    def body(i, carry):
        zt = (me.z + z_order(i)) % 8
        at = pl.ds(pl.multiple_of(zt * 384, 128), 384)
        left = rows_ref[:, :, at].reshape(1024, 384)
        result = dot(left, right(), TN).astype(BF16)
        part[zt] = result.reshape(4, 96, result.shape[-1])
        for copy in core_copy(me, part, core_recv, send_sem, recv_sem, zt, i):
            copy.start()
        return carry

    lax.fori_loop(0, 8, body, 0)


def attention_rows(q, k, v, g, mask):
    factor = 128**-0.5
    s = dot(q, k, NT) * factor
    if mask is not None:
        s = jnp.where(mask, s, -1e30)
    e = jnp.exp(s - jnp.max(s, axis=-1, keepdims=True))
    p = e * (1.0 / jnp.sum(e, axis=-1, keepdims=True))
    dp = dot(g, v, NT)
    inner = jnp.sum(p * dp, axis=-1, keepdims=True)
    ds = (p * (dp - inner) * factor).astype(BF16)
    return dot(ds, k), dot(ds, q, TN), dot(p.astype(BF16), g, TN)


def temporal(h, qkv, grad, dk, dv, out):
    tile = 128
    rows = lax.broadcasted_iota(jnp.int32, (tile, 1024), 0)
    cols = lax.broadcasted_iota(jnp.int32, (tile, 1024), 1)
    mask = (rows % 16) == (cols % 16)

    def body(t, carry):
        at = pl.ds(pl.multiple_of(t * tile, tile), tile)
        one, two, three = attention_rows(
            qkv[0, h, at, :], qkv[1, h], qkv[2, h], grad[h, at, :], mask
        )
        out[at, pl.ds(h * 384, 128)] = one.astype(BF16)
        dk[...] += two
        dv[...] += three
        return carry

    dk[...] = jnp.zeros_like(dk)
    dv[...] = jnp.zeros_like(dv)
    lax.fori_loop(0, 1024 // tile, body, 0)
    out[:, pl.ds(h * 384 + 128, 128)] = dk[...].astype(BF16)
    out[:, pl.ds(h * 384 + 256, 128)] = dv[...].astype(BF16)


def unit_of(y):
    values = y.astype(F32)
    center = values - jnp.mean(values, axis=-1, keepdims=True)
    inverse = lax.rsqrt(jnp.mean(center * center, axis=-1, keepdims=True) + 1e-06)
    return center * inverse, inverse


def main_kernel(
    w_ref, y_ref, res_ref, shift_ref, scale_ref, qkv_ref, grad_ref, sout_ref,
    gso_ref, ig_ref, wt_ref, ws_ref,
    wf, nf, dq, dk, dv, part, from_y, quarter, half, last_y,
    wpart, core_recv, ring, across, igf,
    send_sem, recv_sem, core_send, core_recv_sem,
):
    me = Place()
    net = Net(send_sem, recv_sem)
    s_own = me.yl * 4 + me.x
    far = 1 - me.yl
    meet(me.neighbours(True, True))

    first = gather_pos(net, me, w_ref, wf)
    next(first)

    def norm_tile(i, carry):
        at = pl.ds(pl.multiple_of(i * 16, 16), 16)
        unit, _ = unit_of(y_ref[at, :])
        nf[s_own, at, :] = (unit * (1.0 + scale_ref[...]) + shift_ref[...]).astype(BF16)
        return carry

    lax.fori_loop(0, 8, norm_tile, 0)
    second = gather_seq(net, me, nf, lambda at: None)
    next(second)
    next(first)

    temporal(0, qkv_ref, grad_ref, dk, dv, dq)
    next(second)
    next(first)
    temporal(1, qkv_ref, grad_ref, dk, dv, dq)
    run_all([first, second])

    def partial(x):
        lhs = jnp.concatenate(
            [dq[pl.ds(pl.multiple_of((yl * 4 + x) * 128, 128), 128), :] for yl in range(2)], axis=0
        )

        def body(z, carry):
            w = wf[pl.ds(z * 4, 4), :, pl.ds(0, 768)].reshape(384, 768)
            result = dot(lhs, w, NT).astype(BF16)
            at = pl.ds(pl.multiple_of(z * 384, 128), 384)
            part[x, :, at] = result[:128]
            part[4 + x, :, at] = result[128:]
            return carry

        lax.fori_loop(0, 8, body, 0)

    def h0(yl):
        return lambda x: part.at[yl * 4 + x, pl.ds(0, 64), :]

    def h1(x):
        return part.at[me.yl * 4 + x, pl.ds(64, 64), :]

    def to_partner(x):
        return net.send(
            part.at[far * 4 + x, pl.ds(64, 64), :], from_y.at[x], me.at(yl=far)
        )

    nothing = lambda: None
    swaps = {}
    order = [me.dx(2), me.dx(1), me.dx(-1), me.x]
    partial(order[0])
    keep = {}

    def ready(name):
        def mark():
            keep[name] = True

        return mark

    red_far = reduce_x(net, me, h0(far), quarter.at[0], half.at[0], nothing, ready("far"))
    next(red_far)
    swaps[0] = to_partner(order[0])
    red_own = reduce_x(net, me, h0(me.yl), quarter.at[1], half.at[1], nothing, ready("own"))
    next(red_own)
    for i in range(1, 4):
        partial(order[i])
        swaps[i] = to_partner(order[i])
    next(red_far)
    next(red_own)

    weight_partial(me, nf, lambda: dq[...], wpart, core_recv, core_send, core_recv_sem)
    core = core_copies_of(me, wpart, core_recv, core_send, core_recv_sem)
    wt_steps = reduce_pos_ring(net, me, wpart, core_recv, core, ring, across, wt_ref)

    for i in range(4):
        swaps[i].wait_recv()
        add_into(h1(order[i]), [from_y.at[order[i]]], 64)
        if i == 0:
            red_two = reduce_x(net, me, h1, quarter.at[2], half.at[2], nothing, ready("two"))
            next(red_two)
            next(wt_steps)
    next(red_two)
    for _ in red_far:
        pass
    mine = part.at[far * 4 + me.x, pl.ds(0, 64), :]
    add_into(mine, [half.at[0, 0], half.at[0, 1]], 64)
    swap = net.send(mine, last_y, me.at(yl=far))
    next(wt_steps)
    for _ in red_own:
        pass
    for _ in red_two:
        pass
    swap.wait_recv()

    def back_tile(i, carry, lower):
        base = 0 if lower else 64
        at = pl.ds(pl.multiple_of(i * 16 + base, 16), 16)
        sub = pl.ds(pl.multiple_of(i * 16, 16), 16)
        total = part[s_own, at, :].astype(F32)
        if lower:
            terms = [half.at[1, 0], half.at[1, 1], last_y]
        else:
            terms = [half.at[2, 0], half.at[2, 1]]
        for term in terms:
            total += term[sub, :].astype(F32)
        unit, inverse = unit_of(y_ref[at, :])
        scaled = total * (1.0 + scale_ref[...])
        one = jnp.mean(scaled, axis=-1, keepdims=True)
        two = jnp.mean(scaled * unit, axis=-1, keepdims=True)
        result = res_ref[at, :].astype(F32) + inverse * (scaled - one - unit * two)
        result = result.astype(BF16)
        igf[s_own, at, :] = result
        ig_ref[at, :] = result
        return carry

    lax.fori_loop(0, 4, functools.partial(back_tile, lower=True), 0)
    lax.fori_loop(0, 4, functools.partial(back_tile, lower=False), 0)

    pending = []

    def project(blocks):
        def body(i, carry):
            s = blocks[0]
            for n in range(1, len(blocks)):
                s = jnp.where(i == n, blocks[n], s)
            w = wf[:, :, pl.ds(768, 256)].reshape(3072, 256)
            gso_ref[s] = dot(igf[s], w).astype(BF16)
            return carry

        lax.fori_loop(0, len(blocks), body, 0)

    last = gather_seq(net, me, igf, lambda at: pending.append(at[0] * 4 + at[1]))
    live = [last, wt_steps]
    while live:
        for step in list(live):
            try:
                next(step)
            except StopIteration:
                live.remove(step)
            if len(pending) >= 3 or (step is last and last not in live):
                project(pending)
                pending.clear()

    def ws_tile(z, carry):
        at = pl.ds(pl.multiple_of(z * 384, 128), 384)
        left = igf[:, :, at].reshape(1024, 384)
        for h in range(2):
            ws_ref[z, :, :, pl.ds(h * 128, 128)] = (
                dot(left, sout_ref[h], TN).astype(BF16).reshape(4, 96, 128)
            )
        return carry

    lax.fori_loop(0, 8, ws_tile, 0)
    for pair in core:
        for copy in pair.copies:
            copy.wait_send()
    net.finish()


def ws_kernel(
    part_in, out_ref, part, core_recv, ring, across, send_sem, recv_sem, core_send, core_recv_sem
):
    me = Place()
    net = Net(send_sem, recv_sem)
    meet(me.neighbours(False, True))

    def body(i, carry):
        zt = (me.z + z_order(i)) % 8
        part[zt] = part_in[zt]
        for copy in core_copy(me, part, core_recv, core_send, core_recv_sem, zt, i):
            copy.start()
        return carry

    lax.fori_loop(0, 8, body, 0)
    core = core_copies_of(me, part, core_recv, core_send, core_recv_sem)
    for _ in reduce_pos_ring(net, me, part, core_recv, core, ring, across, out_ref):
        pass
    for pair in core:
        for copy in pair.copies:
            copy.wait_send()
    net.finish()


def spatial_kernel(qkv_ref, grad_ref, out_ref):
    one, two, three = attention_rows(
        qkv_ref[0, 0, 0], qkv_ref[1, 0, 0], qkv_ref[2, 0, 0], grad_ref[0], None
    )
    for c, value in enumerate((one, two, three)):
        out_ref[:, c, 0, 0] = value.astype(BF16).reshape(32, 16, 128)


def vmem():
    return pl.BlockSpec(memory_space=pltpu.VMEM)


def ring_scratch(width):
    return [
        pltpu.VMEM((8, 2, 96, width), BF16),
        pltpu.VMEM((2, 4, 2, 96, width), BF16),
        pltpu.VMEM((96, width), BF16),
    ]


def run_main(w, y, res, shift, scale, qkv, grad, sout):
    dma = pltpu.SemaphoreType.DMA
    return pl.pallas_call(
        main_kernel,
        out_shape=(
            jax.ShapeDtypeStruct((8, 128, 256), BF16),
            jax.ShapeDtypeStruct((128, 3072), BF16),
            jax.ShapeDtypeStruct((96, 768), F32),
            jax.ShapeDtypeStruct((8, 4, 96, 256), BF16),
        ),
        in_specs=[vmem()] * 8,
        out_specs=(vmem(),) * 4,
        scratch_shapes=[
            pltpu.VMEM((32, 96, 1024), BF16),
            pltpu.VMEM((8, 128, 3072), BF16),
            pltpu.VMEM((1024, 768), BF16),
            pltpu.VMEM((1024, 128), F32),
            pltpu.VMEM((1024, 128), F32),
            pltpu.VMEM((8, 128, 3072), BF16),
            pltpu.VMEM((4, 64, 3072), BF16),
            pltpu.VMEM((3, 2, 32, 3072), BF16),
            pltpu.VMEM((3, 2, 64, 3072), BF16),
            pltpu.VMEM((64, 3072), BF16),
            pltpu.VMEM((8, 4, 96, 768), BF16),
            *ring_scratch(768),
            pltpu.VMEM((8, 128, 3072), BF16),
            dma((110,)),
            dma((110,)),
            dma((8, 2)),
            dma((8, 2)),
        ],
        compiler_params=pltpu.CompilerParams(
            collective_id=0, has_side_effects=True, vmem_limit_bytes=63 << 20
        ),
        name="main",
    )(w, y, res, shift, scale, qkv, grad, sout)


def run_ws(part):
    dma = pltpu.SemaphoreType.DMA
    return pl.pallas_call(
        ws_kernel,
        out_shape=jax.ShapeDtypeStruct((96, 256), F32),
        in_specs=[vmem()],
        out_specs=vmem(),
        scratch_shapes=[
            pltpu.VMEM((8, 4, 96, 256), BF16),
            *ring_scratch(256),
            dma((20,)),
            dma((20,)),
            dma((8, 2)),
            dma((8, 2)),
        ],
        compiler_params=pltpu.CompilerParams(
            collective_id=1, has_side_effects=True, vmem_limit_bytes=16 << 20
        ),
        name="ws_sum",
    )(part)


def run_spatial(qkv, grad):
    return pl.pallas_call(
        spatial_kernel,
        grid=(2, 2),
        out_shape=jax.ShapeDtypeStruct((32, 3, 2, 2, 16, 128), BF16),
        in_specs=[
            pl.BlockSpec((3, 1, 1, 512, 128), lambda h, f: (0, h, f, 0, 0)),
            pl.BlockSpec((1, 512, 128), lambda h, f: (f, 0, h)),
        ],
        out_specs=pl.BlockSpec((32, 3, 1, 1, 16, 128), lambda h, f: (0, 0, h, f, 0, 0)),
        compiler_params=pltpu.CompilerParams(vmem_limit_bytes=32 << 20),
        name="spatial",
    )(qkv, grad)


def local(
    y_rows, grad_res, shift, scale_mod, temporal_qkv, temporal_grad,
    spatial_qkv, spatial_out, w_temporal, w_spatial,
):
    w = jnp.concatenate(
        [
            jnp.transpose(w_temporal, (1, 0, 2, 3)).reshape(96, 768),
            jnp.transpose(w_spatial, (1, 0, 2)).reshape(96, 256),
        ],
        axis=1,
    )
    gso, ig, wt, ws_part = run_main(
        w,
        y_rows.reshape(128, 3072),
        grad_res.reshape(128, 3072),
        shift.reshape(1, 3072),
        scale_mod.reshape(1, 3072),
        temporal_qkv.reshape(3, 2, 1024, 128),
        temporal_grad.reshape(2, 1024, 128),
        spatial_out.reshape(2, 1024, 128),
    )
    by_frames = lax.all_to_all(
        gso.reshape(64, 16, 256), "pos", split_axis=0, concat_axis=1, tiled=True
    )
    grads = run_spatial(spatial_qkv, by_frames)
    moved = lax.all_to_all(grads, "pos", split_axis=0, concat_axis=0, tiled=True)
    ws = run_ws(ws_part)
    by_heads = jnp.transpose(moved, (1, 2, 0, 3, 4, 5)).reshape(3, 2, 64, 16, 128)
    wt = jnp.transpose(wt.reshape(96, 2, 3, 128), (1, 0, 2, 3))
    ws = jnp.transpose(ws.reshape(96, 2, 128), (1, 0, 2))
    return by_heads, ig.reshape(8, 16, 3072), wt, ws


def solution(mesh):
    placed = (
        P("seq", "pos", None),
        P("seq", "pos", None),
        P(),
        P(),
        P(None, "seq", None, "pos", None),
        P("seq", None, "pos", None),
        P(None, "seq", "pos", None, None),
        P("seq", None, "pos", None),
        P("seq", "pos", None, None),
        P("seq", "pos", None),
    )
    return jax.shard_map(
        local,
        mesh=mesh,
        in_specs=placed,
        out_specs=(
            P(None, "seq", None, "pos", None),
            P("seq", "pos", None),
            P("seq", "pos", None, None),
            P("seq", "pos", None),
        ),
        check_vma=False,
    )
```

```python
import functools

import jax
import jax.numpy as jnp
from jax import lax
from jax.experimental import pallas as pl
from jax.experimental.pallas import tpu as pltpu
from jax.sharding import PartitionSpec as P

MESH = pl.DeviceIdType.MESH
F32 = jnp.float32
BF16 = jnp.bfloat16
NT = (((1,), (1,)), ((), ()))
TN = (((0,), (0,)), ((), ()))
NN = (((1,), (0,)), ((), ()))


def dot(a, b, dims=NN):
    return lax.dot_general(a, b, dims, preferred_element_type=F32)


class Place:
    def __init__(self):
        s, p = lax.axis_index("seq"), lax.axis_index("pos")
        self.yl, self.x = s // 4, s % 4
        self.z, self.yh, self.co = p // 4, (p // 2) % 2, p % 2

    def at(self, yl=None, x=None, z=None, yh=None, co=None):
        yl = self.yl if yl is None else yl
        x = self.x if x is None else x
        z = self.z if z is None else z
        yh = self.yh if yh is None else yh
        co = self.co if co is None else co
        return (yl * 4 + x, z * 4 + yh * 2 + co)

    def dx(self, k):
        return (self.x + k + 4) % 4

    def dz(self, k):
        return (self.z + k + 8) % 8

    def neighbours(self, seq, pos):
        found = []
        if seq:
            found += [self.at(x=self.dx(1)), self.at(x=self.dx(-1)), self.at(yl=1 - self.yl)]
        if pos:
            found += [
                self.at(z=self.dz(1)),
                self.at(z=self.dz(-1)),
                self.at(yh=1 - self.yh),
                self.at(co=1 - self.co),
            ]
        return found


def meet(devices):
    barrier = pltpu.get_barrier_semaphore()
    for device in devices:
        pl.semaphore_signal(barrier, inc=1, device_id=device, device_id_type=MESH)
    pl.semaphore_wait(barrier, len(devices))


def meet_all(me):
    barrier = pltpu.get_barrier_semaphore()
    for device in me.neighbours(True, False):
        pl.semaphore_signal(barrier, inc=1, device_id=device, device_id_type=MESH)
    s, p = lax.axis_index("seq"), lax.axis_index("pos")

    def body(i, carry):
        pl.semaphore_signal(barrier, inc=1, device_id=(s, (p + i) % 32), device_id_type=MESH)
        return carry

    lax.fori_loop(1, 32, body, 0)
    pl.semaphore_wait(barrier, 34)


class Net:
    def __init__(self, send_sem, recv_sem):
        self.send_sem, self.recv_sem, self.count, self.open = send_sem, recv_sem, 0, []

    def send(self, source, target, device):
        i = self.count
        self.count += 1
        copy = pltpu.make_async_remote_copy(
            src_ref=source,
            dst_ref=target,
            send_sem=self.send_sem.at[i],
            recv_sem=self.recv_sem.at[i],
            device_id=device,
            device_id_type=MESH,
        )
        copy.start()
        self.open.append(copy)
        return copy

    def finish(self):
        for copy in self.open:
            copy.wait_send()
        self.open = []


def run_all(steps):
    live = list(steps)
    while live:
        for step in list(live):
            try:
                next(step)
            except StopIteration:
                live.remove(step)


def add_into(target, terms, rows, tile=16):
    def body(i, carry):
        at = pl.ds(pl.multiple_of(i * tile, tile), tile)
        total = target[at, :].astype(F32)
        for term in terms:
            total += term[at, :].astype(F32)
        target[at, :] = total.astype(BF16)
        return carry

    lax.fori_loop(0, rows // tile, body, 0)


def gather_pos(net, me, own, full):
    def slot(z, r, co):
        return full.at[z * 4 + ((me.yh + r) % 2) * 2 + co]

    up, down = me.at(z=me.dz(1)), me.at(z=me.dz(-1))
    other = me.at(co=1 - me.co)
    mine = slot(me.z, 0, me.co)
    cross = net.send(own, mine, me.at(yh=1 - me.yh))
    plus = [net.send(own, mine, up)]
    minus = [net.send(own, mine, down)]
    cores = [net.send(own, mine, other)]
    mine[...] = own[...]
    yield
    cross.wait_recv()
    near = slot(me.z, 1, me.co)
    plus.append(net.send(near, near, up))
    minus.append(net.send(near, near, down))
    cores.append(net.send(near, near, other))
    yield
    for k in range(1, 5):
        next_plus, next_minus = [], []
        for r in range(2):
            if k < 4 or r == 0:
                plus[r].wait_recv()
                block = slot(me.dz(-k), r, me.co)
                if k < 3 or (k == 3 and r == 0):
                    next_plus.append(net.send(block, block, up))
                else:
                    next_plus.append(None)
                cores.append(net.send(block, block, other))
            if k < 4 or r == 1:
                minus[r].wait_recv()
                block = slot(me.dz(k), r, me.co)
                if k < 3 or (k == 3 and r == 1):
                    next_minus.append(net.send(block, block, down))
                else:
                    next_minus.append(None)
                cores.append(net.send(block, block, other))
        plus, minus = next_plus, next_minus
        yield
    for copy in cores:
        copy.wait_recv()


def gather_seq(net, me, full, done):
    def part(yl, x, first, rows):
        return full.at[yl * 4 + x, pl.ds(first, rows), :]

    yl, x, far = me.yl, me.x, 1 - me.yl
    left, right, xo = me.dx(-1), me.dx(1), me.dx(2)
    to_r, to_l, to_y = me.at(x=right), me.at(x=left), me.at(yl=far)

    def push(block, device):
        return net.send(block, block, device)

    h0, h1 = part(yl, x, 0, 64), part(yl, x, 64, 64)
    y0 = push(h0, to_y)
    r0, l0 = push(h0, to_r), push(h0, to_l)
    y1 = push(h1, to_y)
    r1, l1 = push(h1, to_r), push(h1, to_l)
    done((yl, x))
    yield
    y0.wait_recv()
    f0 = part(far, x, 0, 64)
    rf, lf = push(f0, to_r), push(f0, to_l)
    r0.wait_recv()
    l0.wait_recv()
    ra = push(part(yl, left, 0, 32), to_r)
    lb = push(part(yl, right, 32, 32), to_l)
    y1.wait_recv()
    done((far, x))
    yield
    r1.wait_recv()
    l1.wait_recv()
    rc = push(part(yl, left, 64, 32), to_r)
    ld = push(part(yl, right, 96, 32), to_l)
    yr = push(part(yl, left, 64, 64), to_y)
    yq = push(part(yl, right, 64, 64), to_y)
    done((yl, left))
    done((yl, right))
    yield
    rf.wait_recv()
    lf.wait_recv()
    re = push(part(far, left, 0, 32), to_r)
    lg = push(part(far, right, 32, 32), to_l)
    ra.wait_recv()
    lb.wait_recv()
    yield
    rc.wait_recv()
    ld.wait_recv()
    yo = push(part(yl, xo, 64, 64), to_y)
    done((yl, xo))
    yield
    yr.wait_recv()
    yq.wait_recv()
    done((far, left))
    done((far, right))
    yield
    re.wait_recv()
    lg.wait_recv()
    yo.wait_recv()
    done((far, xo))


def reduce_x(net, me, block, quarter, half, started, result):
    left, right, xo = me.dx(-1), me.dx(1), me.dx(2)
    to_r, to_l = me.at(x=right), me.at(x=left)
    a = net.send(block(xo).at[pl.ds(0, 32)], quarter.at[0], to_r)
    b = net.send(block(xo).at[pl.ds(32, 32)], quarter.at[1], to_l)
    started()
    yield
    a.wait_recv()
    add_into(block(right).at[pl.ds(0, 32)], [quarter.at[0]], 32)
    c = net.send(block(right), half.at[0], to_r)
    b.wait_recv()
    add_into(block(left).at[pl.ds(32, 32)], [quarter.at[1]], 32)
    d = net.send(block(left), half.at[1], to_l)
    yield
    c.wait_recv()
    d.wait_recv()
    result()


def reduce_pos_ring(net, me, part, core_recv, core_copies, ring, across, out):
    up, down = me.at(z=me.dz(1)), me.at(z=me.dz(-1))

    def slot(z, r):
        return part.at[z, ((me.yh + r) % 2) * 2 + me.co]

    def merge(z, k):
        core_copies[k].wait_recv()
        for r in range(2):
            add_into(slot(z, r), [core_recv.at[z, (me.yh + r) % 2]], 96)

    merge(me.dz(4), 0)
    plus = [net.send(slot(me.dz(4), 0), ring.at[0, 0, 0], up), None]
    minus = [None, net.send(slot(me.dz(4), 1), ring.at[1, 0, 1], down)]
    merge(me.dz(3), 1)
    merge(me.dz(-3), 2)
    yield
    for k in range(1, 4):
        next_plus, next_minus = [], []
        for r in range(2):
            at = slot(me.dz(4 - k), r)
            if plus[r] is not None:
                plus[r].wait_recv()
                add_into(at, [ring.at[0, k - 1, r]], 96)
            next_plus.append(net.send(at, ring.at[0, k, r], up))
            at = slot(me.dz(k - 4), r)
            if minus[r] is not None:
                minus[r].wait_recv()
                add_into(at, [ring.at[1, k - 1, r]], 96)
            next_minus.append(net.send(at, ring.at[1, k, r], down))
        plus, minus = next_plus, next_minus
        if k < 3:
            merge(me.dz(3 - k), 2 * k + 1)
            merge(me.dz(k - 3), 2 * k + 2)
        else:
            merge(me.z, 7)
        yield
    for r in (1, 0):
        plus[r].wait_recv()
        minus[r].wait_recv()
        add_into(slot(me.z, r), [ring.at[0, 3, r], ring.at[1, 3, r]], 96)
        if r == 1:
            swap = net.send(slot(me.z, 1), across, me.at(yh=1 - me.yh))
    yield
    swap.wait_recv()
    out[...] = slot(me.z, 0)[...].astype(F32) + across[...].astype(F32)


def z_order(i):
    return 4 + (1 - 2 * (i % 2)) * ((i + 1) // 2)


def core_copy(me, part, core_recv, send_sem, recv_sem, zt, i):
    copies = []
    for yh in range(2):
        copies.append(
            pltpu.make_async_remote_copy(
                src_ref=part.at[zt, yh * 2 + 1 - me.co],
                dst_ref=core_recv.at[zt, yh],
                send_sem=send_sem.at[i, yh],
                recv_sem=recv_sem.at[i, yh],
                device_id=me.at(co=1 - me.co),
                device_id_type=MESH,
            )
        )
    return copies


class Pair:
    def __init__(self, copies):
        self.copies = copies

    def wait_recv(self):
        for copy in self.copies:
            copy.wait_recv()


def core_copies_of(me, part, core_recv, send_sem, recv_sem):
    return [
        Pair(core_copy(me, part, core_recv, send_sem, recv_sem, me.dz(z_order(i) - 8), i))
        for i in range(8)
    ]


def weight_partial(me, rows_ref, right, part, core_recv, send_sem, recv_sem):
    def body(i, carry):
        zt = (me.z + z_order(i)) % 8
        at = pl.ds(pl.multiple_of(zt * 384, 128), 384)
        left = rows_ref[:, :, at].reshape(1024, 384)
        result = dot(left, right(), TN).astype(BF16)
        part[zt] = result.reshape(4, 96, result.shape[-1])
        for copy in core_copy(me, part, core_recv, send_sem, recv_sem, zt, i):
            copy.start()
        return carry

    lax.fori_loop(0, 8, body, 0)


def attention_rows(q, k, v, g, mask):
    factor = 128**-0.5
    s = dot(q, k, NT) * factor
    if mask is not None:
        s = jnp.where(mask, s, -1e30)
    e = jnp.exp(s - jnp.max(s, axis=-1, keepdims=True))
    p = e * (1.0 / jnp.sum(e, axis=-1, keepdims=True))
    dp = dot(g, v, NT)
    inner = jnp.sum(p * dp, axis=-1, keepdims=True)
    ds = (p * (dp - inner) * factor).astype(BF16)
    return dot(ds, k), dot(ds, q, TN), dot(p.astype(BF16), g, TN)


def temporal(h, qkv, grad, dk, dv, out):
    tile = 128
    rows = lax.broadcasted_iota(jnp.int32, (tile, 1024), 0)
    cols = lax.broadcasted_iota(jnp.int32, (tile, 1024), 1)
    mask = (rows % 16) == (cols % 16)

    def body(t, carry):
        at = pl.ds(pl.multiple_of(t * tile, tile), tile)
        one, two, three = attention_rows(
            qkv[0, h, at, :], qkv[1, h], qkv[2, h], grad[h, at, :], mask
        )
        out[at, pl.ds(h * 384, 128)] = one.astype(BF16)
        dk[...] += two
        dv[...] += three
        return carry

    dk[...] = jnp.zeros_like(dk)
    dv[...] = jnp.zeros_like(dv)
    lax.fori_loop(0, 1024 // tile, body, 0)
    out[:, pl.ds(h * 384 + 128, 128)] = dk[...].astype(BF16)
    out[:, pl.ds(h * 384 + 256, 128)] = dv[...].astype(BF16)


def unit_of(y):
    values = y.astype(F32)
    center = values - jnp.mean(values, axis=-1, keepdims=True)
    inverse = lax.rsqrt(jnp.mean(center * center, axis=-1, keepdims=True) + 1e-06)
    return center * inverse, inverse


def main_kernel(
    w_ref, y_ref, res_ref, shift_ref, scale_ref, qkv_ref, grad_ref, sout_ref, sqkv_ref,
    out_ref, ig_ref, wt_ref, ws_ref,
    wf, nf, dq, dk, dv, part, from_y, quarter, half, last_y,
    wpart, core_recv, ring, across, igf,
    gso, byf, gout, wspart, core_recv_s, ring_s, across_s,
    send_sem, recv_sem, core_send, core_recv_sem, core_send_s, core_recv_sem_s,
    gso_send, gso_recv, out_send, out_recv,
):
    me = Place()
    net = Net(send_sem, recv_sem)
    s_own = me.yl * 4 + me.x
    p_own = lax.axis_index("pos")
    far = 1 - me.yl
    meet_all(me)

    first = gather_pos(net, me, w_ref, wf)
    next(first)

    def norm_tile(i, carry):
        at = pl.ds(pl.multiple_of(i * 16, 16), 16)
        unit, _ = unit_of(y_ref[at, :])
        nf[s_own, at, :] = (unit * (1.0 + scale_ref[...]) + shift_ref[...]).astype(BF16)
        return carry

    lax.fori_loop(0, 8, norm_tile, 0)
    second = gather_seq(net, me, nf, lambda at: None)
    next(second)
    next(first)

    temporal(0, qkv_ref, grad_ref, dk, dv, dq)
    next(second)
    next(first)
    temporal(1, qkv_ref, grad_ref, dk, dv, dq)
    run_all([first, second])

    def partial(x):
        lhs = jnp.concatenate(
            [dq[pl.ds(pl.multiple_of((yl * 4 + x) * 128, 128), 128), :] for yl in range(2)], axis=0
        )

        def body(z, carry):
            w = wf[pl.ds(z * 4, 4), :, pl.ds(0, 768)].reshape(384, 768)
            result = dot(lhs, w, NT).astype(BF16)
            at = pl.ds(pl.multiple_of(z * 384, 128), 384)
            part[x, :, at] = result[:128]
            part[4 + x, :, at] = result[128:]
            return carry

        lax.fori_loop(0, 8, body, 0)

    def h0(yl):
        return lambda x: part.at[yl * 4 + x, pl.ds(0, 64), :]

    def h1(x):
        return part.at[me.yl * 4 + x, pl.ds(64, 64), :]

    def to_partner(x):
        return net.send(
            part.at[far * 4 + x, pl.ds(64, 64), :], from_y.at[x], me.at(yl=far)
        )

    nothing = lambda: None
    swaps = {}
    order = [me.dx(2), me.dx(1), me.dx(-1), me.x]
    partial(order[0])
    keep = {}

    def ready(name):
        def mark():
            keep[name] = True

        return mark

    red_far = reduce_x(net, me, h0(far), quarter.at[0], half.at[0], nothing, ready("far"))
    next(red_far)
    swaps[0] = to_partner(order[0])
    red_own = reduce_x(net, me, h0(me.yl), quarter.at[1], half.at[1], nothing, ready("own"))
    next(red_own)
    for i in range(1, 4):
        partial(order[i])
        swaps[i] = to_partner(order[i])
    next(red_far)
    next(red_own)

    weight_partial(me, nf, lambda: dq[...], wpart, core_recv, core_send, core_recv_sem)
    core = core_copies_of(me, wpart, core_recv, core_send, core_recv_sem)
    wt_steps = reduce_pos_ring(net, me, wpart, core_recv, core, ring, across, wt_ref)

    for i in range(4):
        swaps[i].wait_recv()
        add_into(h1(order[i]), [from_y.at[order[i]]], 64)
        if i == 0:
            red_two = reduce_x(net, me, h1, quarter.at[2], half.at[2], nothing, ready("two"))
            next(red_two)
            next(wt_steps)
    next(red_two)
    for _ in red_far:
        pass
    mine = part.at[far * 4 + me.x, pl.ds(0, 64), :]
    add_into(mine, [half.at[0, 0], half.at[0, 1]], 64)
    swap = net.send(mine, last_y, me.at(yl=far))
    next(wt_steps)
    for _ in red_own:
        pass
    for _ in red_two:
        pass
    swap.wait_recv()

    def back_tile(i, carry, lower):
        base = 0 if lower else 64
        at = pl.ds(pl.multiple_of(i * 16 + base, 16), 16)
        sub = pl.ds(pl.multiple_of(i * 16, 16), 16)
        total = part[s_own, at, :].astype(F32)
        if lower:
            terms = [half.at[1, 0], half.at[1, 1], last_y]
        else:
            terms = [half.at[2, 0], half.at[2, 1]]
        for term in terms:
            total += term[sub, :].astype(F32)
        unit, inverse = unit_of(y_ref[at, :])
        scaled = total * (1.0 + scale_ref[...])
        one = jnp.mean(scaled, axis=-1, keepdims=True)
        two = jnp.mean(scaled * unit, axis=-1, keepdims=True)
        result = res_ref[at, :].astype(F32) + inverse * (scaled - one - unit * two)
        result = result.astype(BF16)
        igf[s_own, at, :] = result
        ig_ref[at, :] = result
        return carry

    lax.fori_loop(0, 4, functools.partial(back_tile, lower=True), 0)
    lax.fori_loop(0, 4, functools.partial(back_tile, lower=False), 0)

    def gso_copy(p_to, p_from):
        return pltpu.make_async_remote_copy(
            src_ref=gso.at[p_to],
            dst_ref=byf.at[p_from],
            send_sem=gso_send.at[p_to],
            recv_sem=gso_recv.at[p_from],
            device_id=(s_own, p_to),
            device_id_type=MESH,
        )

    def project(blocks):
        def body(i, carry):
            s = blocks[0]
            for n in range(1, len(blocks)):
                s = jnp.where(i == n, blocks[n], s)
            w = wf[:, :, pl.ds(768, 256)].reshape(3072, 256)
            result = dot(igf[s], w).astype(BF16).reshape(4, 32, 256)
            gso[pl.ds(s * 4, 4)] = result
            for n in range(4):
                p_to = s * 4 + n

                @pl.when(p_to == p_own)
                def _():
                    byf[p_to] = result[n]

                @pl.when(p_to != p_own)
                def _():
                    gso_copy(p_to, p_own).start()

            return carry

        lax.fori_loop(0, len(blocks), body, 0)

    pending = []
    last = gather_seq(net, me, igf, lambda at: pending.append(at[0] * 4 + at[1]))
    live = [last, wt_steps]
    while live:
        for step in list(live):
            try:
                next(step)
            except StopIteration:
                live.remove(step)
            if pending:
                project(pending)
                pending.clear()

    weight_partial(
        me, igf, lambda: sout_ref[...], wspart, core_recv_s, core_send_s, core_recv_sem_s
    )
    core_s = core_copies_of(me, wspart, core_recv_s, core_send_s, core_recv_sem_s)
    ws_steps = reduce_pos_ring(
        net, me, wspart, core_recv_s, core_s, ring_s, across_s, ws_ref
    )
    next(ws_steps)

    def others(body):
        def step(i, carry):
            body((p_own + i) % 32)
            return carry

        lax.fori_loop(1, 32, step, 0)

    others(lambda p: gso_copy(p_own, p).wait_recv())

    def out_copy(h, p_to, p_from):
        return pltpu.make_async_remote_copy(
            src_ref=gout.at[p_to, h],
            dst_ref=out_ref.at[:, h, p_from],
            send_sem=out_send.at[h, p_to],
            recv_sem=out_recv.at[h, p_from],
            device_id=(s_own, p_to),
            device_id_type=MESH,
        )

    for h in range(2):
        spatial(h, sqkv_ref, byf, dk, dv, gout)
        out_ref[:, h, p_own] = gout[p_own, h]
        others(lambda p: out_copy(h, p, p_own).start())
        next(ws_steps)
    for _ in ws_steps:
        pass
    for h in range(2):
        others(lambda p: out_copy(h, p_own, p).wait_recv())
    for h in range(2):
        others(lambda p: out_copy(h, p, p_own).wait_send())
    others(lambda p: gso_copy(p, p_own).wait_send())
    for pair in core + core_s:
        for copy in pair.copies:
            copy.wait_send()
    net.finish()


def spatial(h, qkv, byf, dk, dv, gout):
    tile = 256

    def frame(f, carry):
        def rows(t, inner):
            at = pl.ds(pl.multiple_of(t * tile, tile), tile)
            blocks = pl.ds(t * (tile // 16), tile // 16)
            g = byf[blocks, pl.ds(f * 16, 16), pl.ds(h * 128, 128)].reshape(tile, 128)
            one, two, three = attention_rows(
                qkv[0, h, f, at, :], qkv[1, h, f], qkv[2, h, f], g, None
            )
            gout[blocks, h, 0, f] = one.astype(BF16).reshape(tile // 16, 16, 128)
            dk[:512] += two
            dv[:512] += three
            return inner

        dk[:512] = jnp.zeros((512, 128), F32)
        dv[:512] = jnp.zeros((512, 128), F32)
        lax.fori_loop(0, 512 // tile, rows, 0)
        gout[:, h, 1, f] = dk[:512].astype(BF16).reshape(32, 16, 128)
        gout[:, h, 2, f] = dv[:512].astype(BF16).reshape(32, 16, 128)
        return carry

    lax.fori_loop(0, 2, frame, 0)


def vmem():
    return pl.BlockSpec(memory_space=pltpu.VMEM)


def ring_scratch(width):
    return [
        pltpu.VMEM((8, 2, 96, width), BF16),
        pltpu.VMEM((2, 4, 2, 96, width), BF16),
        pltpu.VMEM((96, width), BF16),
    ]


def run_main(w, y, res, shift, scale, qkv, grad, sout, sqkv):
    dma = pltpu.SemaphoreType.DMA
    return pl.pallas_call(
        main_kernel,
        out_shape=(
            jax.ShapeDtypeStruct((3, 2, 32, 2, 16, 128), BF16),
            jax.ShapeDtypeStruct((128, 3072), BF16),
            jax.ShapeDtypeStruct((96, 768), F32),
            jax.ShapeDtypeStruct((96, 256), F32),
        ),
        in_specs=[vmem()] * 9,
        out_specs=(vmem(),) * 4,
        scratch_shapes=[
            pltpu.VMEM((32, 96, 1024), BF16),
            pltpu.VMEM((8, 128, 3072), BF16),
            pltpu.VMEM((1024, 768), BF16),
            pltpu.VMEM((1024, 128), F32),
            pltpu.VMEM((1024, 128), F32),
            pltpu.VMEM((8, 128, 3072), BF16),
            pltpu.VMEM((4, 64, 3072), BF16),
            pltpu.VMEM((3, 2, 32, 3072), BF16),
            pltpu.VMEM((3, 2, 64, 3072), BF16),
            pltpu.VMEM((64, 3072), BF16),
            pltpu.VMEM((8, 4, 96, 768), BF16),
            *ring_scratch(768),
            pltpu.VMEM((8, 128, 3072), BF16),
            pltpu.VMEM((32, 32, 256), BF16),
            pltpu.VMEM((32, 32, 256), BF16),
            pltpu.VMEM((32, 2, 3, 2, 16, 128), BF16),
            pltpu.VMEM((8, 4, 96, 256), BF16),
            *ring_scratch(256),
            dma((130,)),
            dma((130,)),
            dma((8, 2)),
            dma((8, 2)),
            dma((8, 2)),
            dma((8, 2)),
            dma((32,)),
            dma((32,)),
            dma((2, 32)),
            dma((2, 32)),
        ],
        compiler_params=pltpu.CompilerParams(
            collective_id=0, has_side_effects=True, vmem_limit_bytes=63 << 20
        ),
        name="main",
    )(w, y, res, shift, scale, qkv, grad, sout, sqkv)


def local(
    y_rows, grad_res, shift, scale_mod, temporal_qkv, temporal_grad,
    spatial_qkv, spatial_out, w_temporal, w_spatial,
):
    w = jnp.concatenate(
        [
            jnp.transpose(w_temporal, (1, 0, 2, 3)).reshape(96, 768),
            jnp.transpose(w_spatial, (1, 0, 2)).reshape(96, 256),
        ],
        axis=1,
    )
    grads, ig, wt, ws = run_main(
        w,
        y_rows.reshape(128, 3072),
        grad_res.reshape(128, 3072),
        shift.reshape(1, 3072),
        scale_mod.reshape(1, 3072),
        temporal_qkv.reshape(3, 2, 1024, 128),
        temporal_grad.reshape(2, 1024, 128),
        jnp.transpose(spatial_out, (1, 2, 0, 3)).reshape(1024, 256),
        spatial_qkv,
    )
    by_heads = grads.reshape(3, 2, 64, 16, 128)
    wt = jnp.transpose(wt.reshape(96, 2, 3, 128), (1, 0, 2, 3))
    ws = jnp.transpose(ws.reshape(96, 2, 128), (1, 0, 2))
    return by_heads, ig.reshape(8, 16, 3072), wt, ws


def solution(mesh):
    placed = (
        P("seq", "pos", None),
        P("seq", "pos", None),
        P(),
        P(),
        P(None, "seq", None, "pos", None),
        P("seq", None, "pos", None),
        P(None, "seq", "pos", None, None),
        P("seq", None, "pos", None),
        P("seq", "pos", None, None),
        P("seq", "pos", None),
    )
    return jax.shard_map(
        local,
        mesh=mesh,
        in_specs=placed,
        out_specs=(
            P(None, "seq", None, "pos", None),
            P("seq", "pos", None),
            P("seq", "pos", None, None),
            P("seq", "pos", None),
        ),
        check_vma=False,
    )
```

```python
import functools

import jax
import jax.numpy as jnp
from jax import lax
from jax.experimental import pallas as pl
from jax.experimental.pallas import tpu as pltpu
from jax.sharding import PartitionSpec as P

MESH = pl.DeviceIdType.MESH
F32 = jnp.float32
BF16 = jnp.bfloat16
NT = (((1,), (1,)), ((), ()))
TN = (((0,), (0,)), ((), ()))
NN = (((1,), (0,)), ((), ()))


def dot(a, b, dims=NN):
    return lax.dot_general(a, b, dims, preferred_element_type=F32)


class Place:
    def __init__(self):
        s, p = lax.axis_index("seq"), lax.axis_index("pos")
        self.yl, self.x = s // 4, s % 4
        self.z, self.yh, self.co = p // 4, (p // 2) % 2, p % 2

    def at(self, yl=None, x=None, z=None, yh=None, co=None):
        yl = self.yl if yl is None else yl
        x = self.x if x is None else x
        z = self.z if z is None else z
        yh = self.yh if yh is None else yh
        co = self.co if co is None else co
        return (yl * 4 + x, z * 4 + yh * 2 + co)

    def dx(self, k):
        return (self.x + k + 4) % 4

    def dz(self, k):
        return (self.z + k + 8) % 8

    def neighbours(self, seq, pos):
        found = []
        if seq:
            found += [self.at(x=self.dx(1)), self.at(x=self.dx(-1)), self.at(yl=1 - self.yl)]
        if pos:
            found += [
                self.at(z=self.dz(1)),
                self.at(z=self.dz(-1)),
                self.at(yh=1 - self.yh),
                self.at(co=1 - self.co),
            ]
        return found


def meet(devices):
    barrier = pltpu.get_barrier_semaphore()
    for device in devices:
        pl.semaphore_signal(barrier, inc=1, device_id=device, device_id_type=MESH)
    pl.semaphore_wait(barrier, len(devices))


class Net:
    def __init__(self, send_sem, recv_sem):
        self.send_sem, self.recv_sem, self.count, self.open = send_sem, recv_sem, 0, []

    def send(self, source, target, device):
        i = self.count
        self.count += 1
        copy = pltpu.make_async_remote_copy(
            src_ref=source,
            dst_ref=target,
            send_sem=self.send_sem.at[i],
            recv_sem=self.recv_sem.at[i],
            device_id=device,
            device_id_type=MESH,
        )
        copy.start()
        self.open.append(copy)
        return copy

    def finish(self):
        for copy in self.open:
            copy.wait_send()
        self.open = []


def add_into(target, terms, rows, tile=16):
    def body(i, carry):
        at = pl.ds(pl.multiple_of(i * tile, tile), tile)
        total = target[at, :].astype(F32)
        for term in terms:
            total += term[at, :].astype(F32)
        target[at, :] = total.astype(BF16)
        return carry

    lax.fori_loop(0, rows // tile, body, 0)


def gather_pos(net, me, full):
    def slot(z, r, co):
        return full.at[z * 4 + ((me.yh + r) % 2) * 2 + co]

    up, down = me.at(z=me.dz(1)), me.at(z=me.dz(-1))
    other = me.at(co=1 - me.co)
    mine = slot(me.z, 0, me.co)
    cross = net.send(mine, mine, me.at(yh=1 - me.yh))
    plus = [net.send(mine, mine, up)]
    minus = [net.send(mine, mine, down)]
    cores = [net.send(mine, mine, other)]
    yield
    cross.wait_recv()
    near = slot(me.z, 1, me.co)
    plus.append(net.send(near, near, up))
    minus.append(net.send(near, near, down))
    cores.append(net.send(near, near, other))
    yield
    for k in range(1, 5):
        next_plus, next_minus = [], []
        for r in range(2):
            if k < 4 or r == 0:
                plus[r].wait_recv()
                block = slot(me.dz(-k), r, me.co)
                if k < 3 or (k == 3 and r == 0):
                    next_plus.append(net.send(block, block, up))
                else:
                    next_plus.append(None)
                cores.append(net.send(block, block, other))
            if k < 4 or r == 1:
                minus[r].wait_recv()
                block = slot(me.dz(k), r, me.co)
                if k < 3 or (k == 3 and r == 1):
                    next_minus.append(net.send(block, block, down))
                else:
                    next_minus.append(None)
                cores.append(net.send(block, block, other))
            if k < 4:
                yield
        plus, minus = next_plus, next_minus
    yield
    for copy in cores:
        copy.wait_recv()


def gather_seq(net, me, full, done):
    def part(yl, x, first, rows):
        return full.at[yl * 4 + x, pl.ds(first, rows), :]

    yl, x, far = me.yl, me.x, 1 - me.yl
    left, right, xo = me.dx(-1), me.dx(1), me.dx(2)
    to_r, to_l, to_y = me.at(x=right), me.at(x=left), me.at(yl=far)

    def push(block, device):
        return net.send(block, block, device)

    h0, h1 = part(yl, x, 0, 64), part(yl, x, 64, 64)
    y0 = push(h0, to_y)
    r0, l0 = push(h0, to_r), push(h0, to_l)
    y1 = push(h1, to_y)
    r1, l1 = push(h1, to_r), push(h1, to_l)
    done((yl, x))
    yield
    y0.wait_recv()
    f0 = part(far, x, 0, 64)
    rf, lf = push(f0, to_r), push(f0, to_l)
    r0.wait_recv()
    l0.wait_recv()
    ra = push(part(yl, left, 0, 32), to_r)
    lb = push(part(yl, right, 32, 32), to_l)
    y1.wait_recv()
    done((far, x))
    yield
    r1.wait_recv()
    l1.wait_recv()
    rc = push(part(yl, left, 64, 32), to_r)
    ld = push(part(yl, right, 96, 32), to_l)
    yr = push(part(yl, left, 64, 64), to_y)
    yq = push(part(yl, right, 64, 64), to_y)
    done((yl, left))
    done((yl, right))
    yield
    rf.wait_recv()
    lf.wait_recv()
    re = push(part(far, left, 0, 32), to_r)
    lg = push(part(far, right, 32, 32), to_l)
    ra.wait_recv()
    lb.wait_recv()
    yield
    rc.wait_recv()
    ld.wait_recv()
    yo = push(part(yl, xo, 64, 64), to_y)
    done((yl, xo))
    yield
    yr.wait_recv()
    yq.wait_recv()
    done((far, left))
    done((far, right))
    yield
    re.wait_recv()
    lg.wait_recv()
    yo.wait_recv()
    done((far, xo))


def reduce_x(net, me, block, quarter, half, started, result):
    left, right, xo = me.dx(-1), me.dx(1), me.dx(2)
    to_r, to_l = me.at(x=right), me.at(x=left)
    a = net.send(block(xo).at[pl.ds(0, 32)], quarter.at[0], to_r)
    b = net.send(block(xo).at[pl.ds(32, 32)], quarter.at[1], to_l)
    started()
    yield
    a.wait_recv()
    add_into(block(right).at[pl.ds(0, 32)], [quarter.at[0]], 32)
    c = net.send(block(right), half.at[0], to_r)
    b.wait_recv()
    add_into(block(left).at[pl.ds(32, 32)], [quarter.at[1]], 32)
    d = net.send(block(left), half.at[1], to_l)
    yield
    c.wait_recv()
    d.wait_recv()
    result()


def reduce_pos_ring(net, me, part, core_recv, core_copies, ring, across, out):
    up, down = me.at(z=me.dz(1)), me.at(z=me.dz(-1))

    def slot(z, r):
        return part.at[z, ((me.yh + r) % 2) * 2 + me.co]

    def merge(z, k):
        core_copies[k].wait_recv()
        for r in range(2):
            add_into(slot(z, r), [core_recv.at[z, (me.yh + r) % 2]], 96)

    merge(me.dz(4), 0)
    plus = [net.send(slot(me.dz(4), 0), ring.at[0, 0, 0], up), None]
    minus = [None, net.send(slot(me.dz(4), 1), ring.at[1, 0, 1], down)]
    merge(me.dz(3), 1)
    merge(me.dz(-3), 2)
    yield
    for k in range(1, 4):
        next_plus, next_minus = [], []
        for r in range(2):
            at = slot(me.dz(4 - k), r)
            if plus[r] is not None:
                plus[r].wait_recv()
                add_into(at, [ring.at[0, k - 1, r]], 96)
            next_plus.append(net.send(at, ring.at[0, k, r], up))
            at = slot(me.dz(k - 4), r)
            if minus[r] is not None:
                minus[r].wait_recv()
                add_into(at, [ring.at[1, k - 1, r]], 96)
            next_minus.append(net.send(at, ring.at[1, k, r], down))
        plus, minus = next_plus, next_minus
        if k < 3:
            merge(me.dz(3 - k), 2 * k + 1)
            merge(me.dz(k - 3), 2 * k + 2)
        else:
            merge(me.z, 7)
        yield
    for r in (1, 0):
        plus[r].wait_recv()
        minus[r].wait_recv()
        add_into(slot(me.z, r), [ring.at[0, 3, r], ring.at[1, 3, r]], 96)
        if r == 1:
            swap = net.send(slot(me.z, 1), across, me.at(yh=1 - me.yh))
    yield
    swap.wait_recv()
    out(slot(me.z, 0)[...].astype(F32) + across[...].astype(F32))


def reduce_pos_direct(net, me, part, core_recv, core_copies, from_yh, from_z, out):
    def slot(z, r):
        return part.at[z, ((me.yh + r) % 2) * 2 + me.co]

    for i in range(8):
        core_copies[i].wait_recv()

    def merge(z, carry):
        for r in range(2):
            add_into(slot(z, r), [core_recv.at[z, (me.yh + r) % 2]], 96)
        return carry

    lax.fori_loop(0, 8, merge, 0)
    swap = net.send(
        part.at[:, (1 - me.yh) * 2 + me.co], from_yh, me.at(yh=1 - me.yh)
    )
    yield
    swap.wait_recv()

    def join(z, carry):
        add_into(slot(z, 0), [from_yh.at[z]], 96)
        return carry

    lax.fori_loop(0, 8, join, 0)
    copies = [
        net.send(slot(me.dz(k), 0), from_z.at[me.z], me.at(z=me.dz(k)))
        for k in (4, 3, 5, 2, 6, 1, 7)
    ]
    yield
    for copy in copies:
        copy.wait_recv()
    total = slot(me.z, 0)[...].astype(F32)
    for k in range(1, 8):
        total += from_z[me.dz(k)].astype(F32)
    out(total)


def z_order(i):
    return 4 + (1 - 2 * (i % 2)) * ((i + 1) // 2)


def core_copy(me, part, core_recv, send_sem, recv_sem, zt, i):
    copies = []
    for yh in range(2):
        copies.append(
            pltpu.make_async_remote_copy(
                src_ref=part.at[zt, yh * 2 + 1 - me.co],
                dst_ref=core_recv.at[zt, yh],
                send_sem=send_sem.at[i, yh],
                recv_sem=recv_sem.at[i, yh],
                device_id=me.at(co=1 - me.co),
                device_id_type=MESH,
            )
        )
    return copies


class Pair:
    def __init__(self, copies):
        self.copies = copies

    def wait_recv(self):
        for copy in self.copies:
            copy.wait_recv()


def core_copies_of(me, part, core_recv, send_sem, recv_sem):
    return [
        Pair(core_copy(me, part, core_recv, send_sem, recv_sem, me.dz(z_order(i) - 8), i))
        for i in range(8)
    ]


def weight_partial(me, rows_ref, right, part, core_recv, send_sem, recv_sem):
    def body(i, carry):
        zt = (me.z + z_order(i)) % 8
        at = pl.ds(pl.multiple_of(zt * 384, 128), 384)
        left = rows_ref[:, :, at].reshape(1024, 384)
        result = dot(left, right(), TN).astype(BF16)
        part[zt] = result.reshape(4, 96, result.shape[-1])
        for copy in core_copy(me, part, core_recv, send_sem, recv_sem, zt, i):
            copy.start()
        return carry

    lax.fori_loop(0, 8, body, 0)


def attention_rows(q, k, v, g, mask):
    factor = 128**-0.5
    s = dot(q, k, NT) * factor
    if mask is not None:
        s = jnp.where(mask, s, -1e30)
    e = jnp.exp(s - jnp.max(s, axis=-1, keepdims=True))
    p = e * (1.0 / jnp.sum(e, axis=-1, keepdims=True))
    dp = dot(g, v, NT)
    inner = jnp.sum(p * dp, axis=-1, keepdims=True)
    ds = (p * (dp - inner) * factor).astype(BF16)
    return dot(ds, k), dot(ds, q, TN), dot(p.astype(BF16), g, TN)


def temporal(h, qkv, grad, dk, dv, out):
    tile = 128
    rows = lax.broadcasted_iota(jnp.int32, (tile, 1024), 0)
    cols = lax.broadcasted_iota(jnp.int32, (tile, 1024), 1)
    mask = (rows % 16) == (cols % 16)

    def body(t, carry):
        at = pl.ds(pl.multiple_of(t * tile, tile), tile)
        one, two, three = attention_rows(
            qkv[0, h, at, :], qkv[1, h], qkv[2, h], grad[h, at, :], mask
        )
        out[at, pl.ds(h * 384, 128)] = one.astype(BF16)
        dk[...] += two
        dv[...] += three
        return carry

    dk[...] = jnp.zeros_like(dk)
    dv[...] = jnp.zeros_like(dv)
    lax.fori_loop(0, 1024 // tile, body, 0)
    out[:, pl.ds(h * 384 + 128, 128)] = dk[...].astype(BF16)
    out[:, pl.ds(h * 384 + 256, 128)] = dv[...].astype(BF16)


def unit_of(y):
    values = y.astype(F32)
    center = values - jnp.mean(values, axis=-1, keepdims=True)
    inverse = lax.rsqrt(jnp.mean(center * center, axis=-1, keepdims=True) + 1e-06)
    return center * inverse, inverse


def main_kernel(
    w_ref, v_ref, y_ref, res_ref, shift_ref, scale_ref, qkv_ref, grad_ref, sout_ref, sqkv_ref,
    out_ref, ig_ref, wt_ref, ws_ref,
    wf, nf, dq, dk, dv, part, from_y, quarter, half, last_y,
    wpart, core_recv, ring, across, igf,
    gso, byf, gout, wspart, core_recv_s, from_yh, from_z,
    send_sem, recv_sem, core_send, core_recv_sem, core_send_s, core_recv_sem_s,
    gso_send, gso_recv, out_send, out_recv,
    qkv, grad, res, sout, sqkv, local_sem,
):
    me = Place()
    net = Net(send_sem, recv_sem)
    s_own = me.yl * 4 + me.x
    p_own = lax.axis_index("pos")
    far = 1 - me.yl
    local_copies = [
        pltpu.make_async_copy(source, target, local_sem.at[i])
        for i, (source, target) in enumerate(
            [(qkv_ref, qkv), (grad_ref, grad), (res_ref, res), (sout_ref, sout), (sqkv_ref, sqkv)]
        )
    ]
    for copy in local_copies:
        copy.start()
    meet(me.neighbours(True, True))

    def norm_tile(i, carry):
        at = pl.ds(pl.multiple_of(i * 16, 16), 16)
        unit, _ = unit_of(y_ref[at, :])
        nf[s_own, at, :] = (unit * (1.0 + scale_ref[...]) + shift_ref[...]).astype(BF16)
        return carry

    for h in range(2):
        for c in range(3):
            wf[p_own, :, pl.ds((h * 3 + c) * 128, 128)] = w_ref[h, c]
        wf[p_own, :, pl.ds(768 + h * 128, 128)] = v_ref[h]
    first = gather_pos(net, me, wf)
    second = gather_seq(net, me, nf, lambda at: None)
    next(first)
    lax.fori_loop(0, 8, norm_tile, 0)
    next(second)
    for copy in local_copies[:2]:
        copy.wait()
    temporal(0, qkv, grad, dk, dv, dq)
    next(first)
    next(first)
    temporal(1, qkv, grad, dk, dv, dq)
    next(first)
    next(first)
    next(second)
    next(second)
    next(first)
    next(first)
    next(first)
    next(second)
    next(second)
    for _ in first:
        pass

    def partial(x):
        lhs = jnp.concatenate(
            [dq[pl.ds(pl.multiple_of((yl * 4 + x) * 128, 128), 128), :] for yl in range(2)], axis=0
        )

        def body(z, carry):
            w = wf[pl.ds(z * 4, 4), :, pl.ds(0, 768)].reshape(384, 768)
            result = dot(lhs, w, NT).astype(BF16)
            at = pl.ds(pl.multiple_of(z * 384, 128), 384)
            part[x, :, at] = result[:128]
            part[4 + x, :, at] = result[128:]
            return carry

        lax.fori_loop(0, 8, body, 0)

    def h0(yl):
        return lambda x: part.at[yl * 4 + x, pl.ds(0, 64), :]

    def h1(x):
        return part.at[me.yl * 4 + x, pl.ds(64, 64), :]

    def to_partner(x):
        return net.send(
            part.at[far * 4 + x, pl.ds(64, 64), :], from_y.at[x], me.at(yl=far)
        )

    nothing = lambda: None
    swaps = {}
    order = [me.dx(2), me.dx(1), me.dx(-1), me.x]
    partial(order[0])
    keep = {}

    def ready(name):
        def mark():
            keep[name] = True

        return mark

    red_far = reduce_x(net, me, h0(far), quarter.at[0], half.at[0], nothing, ready("far"))
    next(red_far)
    swaps[0] = to_partner(order[0])
    red_own = reduce_x(net, me, h0(me.yl), quarter.at[1], half.at[1], nothing, ready("own"))
    next(red_own)
    for i in range(1, 4):
        partial(order[i])
        swaps[i] = to_partner(order[i])
    next(red_far)
    next(red_own)

    for _ in second:
        pass
    weight_partial(me, nf, lambda: dq[...], wpart, core_recv, core_send, core_recv_sem)
    core = core_copies_of(me, wpart, core_recv, core_send, core_recv_sem)

    def wt_total(value):
        for h in range(2):
            for c in range(3):
                wt_ref[h, c] = value[:, (h * 3 + c) * 128 : (h * 3 + c + 1) * 128]

    def ws_total(value):
        for h in range(2):
            ws_ref[h] = value[:, h * 128 : (h + 1) * 128]

    wt_steps = reduce_pos_ring(net, me, wpart, core_recv, core, ring, across, wt_total)

    for i in range(4):
        swaps[i].wait_recv()
        add_into(h1(order[i]), [from_y.at[order[i]]], 64)
        if i == 0:
            red_two = reduce_x(net, me, h1, quarter.at[2], half.at[2], nothing, ready("two"))
            next(red_two)
            next(wt_steps)
    next(red_two)
    for _ in red_far:
        pass
    mine = part.at[far * 4 + me.x, pl.ds(0, 64), :]
    add_into(mine, [half.at[0, 0], half.at[0, 1]], 64)
    swap = net.send(mine, last_y, me.at(yl=far))
    next(wt_steps)
    for _ in red_own:
        pass
    for _ in red_two:
        pass
    swap.wait_recv()

    for copy in local_copies[2:]:
        copy.wait()

    def back_tile(i, carry, lower):
        base = 0 if lower else 64
        at = pl.ds(pl.multiple_of(i * 16 + base, 16), 16)
        sub = pl.ds(pl.multiple_of(i * 16, 16), 16)
        total = part[s_own, at, :].astype(F32)
        if lower:
            terms = [half.at[1, 0], half.at[1, 1], last_y]
        else:
            terms = [half.at[2, 0], half.at[2, 1]]
        for term in terms:
            total += term[sub, :].astype(F32)
        unit, inverse = unit_of(y_ref[at, :])
        scaled = total * (1.0 + scale_ref[...])
        one = jnp.mean(scaled, axis=-1, keepdims=True)
        two = jnp.mean(scaled * unit, axis=-1, keepdims=True)
        result = res[at, :].astype(F32) + inverse * (scaled - one - unit * two)
        result = result.astype(BF16)
        igf[s_own, at, :] = result
        ig_ref[at, :] = result
        return carry

    lax.fori_loop(0, 4, functools.partial(back_tile, lower=True), 0)
    lax.fori_loop(0, 4, functools.partial(back_tile, lower=False), 0)

    def gso_copy(p_to, p_from):
        return pltpu.make_async_remote_copy(
            src_ref=gso.at[p_to],
            dst_ref=byf.at[p_from],
            send_sem=gso_send.at[p_to],
            recv_sem=gso_recv.at[p_from],
            device_id=(s_own, p_to),
            device_id_type=MESH,
        )

    def project(blocks):
        def body(i, carry):
            s = blocks[0]
            for n in range(1, len(blocks)):
                s = jnp.where(i == n, blocks[n], s)
            w = wf[:, :, pl.ds(768, 256)].reshape(3072, 256)
            result = dot(igf[s], w).astype(BF16).reshape(4, 32, 256)
            gso[pl.ds(s * 4, 4)] = result
            for n in range(4):
                p_to = s * 4 + n

                @pl.when(p_to == p_own)
                def _():
                    byf[p_to] = result[n]

                @pl.when(p_to != p_own)
                def _():
                    gso_copy(p_to, p_own).start()

            return carry

        lax.fori_loop(0, len(blocks), body, 0)

    def others(body):
        def step(i, carry):
            body((p_own + i) % 32)
            return carry

        lax.fori_loop(1, 32, step, 0)

    def out_copy(h, p_to, p_from):
        return pltpu.make_async_remote_copy(
            src_ref=gout.at[p_to, h],
            dst_ref=out_ref.at[:, h, p_from],
            send_sem=out_send.at[h, p_to],
            recv_sem=out_recv.at[h, p_from],
            device_id=(s_own, p_to),
            device_id_type=MESH,
        )

    def attend(h):
        if h == 0:
            others(lambda p: gso_copy(p_own, p).wait_recv())
        spatial(h, sqkv, byf, dk, dv, gout)
        out_ref[:, h, p_own] = gout[p_own, h]
        others(lambda p: out_copy(h, p, p_own).start())

    pending = []

    def come():
        blocks = list(pending)
        pending.clear()
        project(blocks)
        return blocks

    last = gather_seq(net, me, igf, lambda at: pending.append(at[0] * 4 + at[1]))
    next(last)
    come()
    next(wt_steps)
    next(last)
    next(last)
    come()
    next(wt_steps)
    next(last)
    next(last)
    come()
    for _ in wt_steps:
        pass
    next(last)
    come()
    for _ in last:
        pass
    come()

    weight_partial(
        me,
        igf,
        lambda: jnp.concatenate([sout[0], sout[1]], axis=1),
        wspart,
        core_recv_s,
        core_send_s,
        core_recv_sem_s,
    )
    core_s = core_copies_of(me, wspart, core_recv_s, core_send_s, core_recv_sem_s)
    ws_steps = reduce_pos_direct(
        net, me, wspart, core_recv_s, core_s, from_yh, from_z, ws_total
    )
    next(ws_steps)
    for h in range(2):
        attend(h)
        next(ws_steps, None)
    for _ in ws_steps:
        pass
    for h in range(2):
        others(lambda p: out_copy(h, p_own, p).wait_recv())
    for h in range(2):
        others(lambda p: out_copy(h, p, p_own).wait_send())
    others(lambda p: gso_copy(p, p_own).wait_send())
    for pair in core + core_s:
        for copy in pair.copies:
            copy.wait_send()
    net.finish()


def spatial(h, qkv, byf, dk, dv, gout):
    tile = 256

    def frame(f, carry):
        def rows(t, inner):
            at = pl.ds(pl.multiple_of(t * tile, tile), tile)
            blocks = pl.ds(t * (tile // 16), tile // 16)
            g = byf[blocks, pl.ds(f * 16, 16), pl.ds(h * 128, 128)].reshape(tile, 128)
            one, two, three = attention_rows(
                qkv[0, h, f, at, :], qkv[1, h, f], qkv[2, h, f], g, None
            )
            gout[blocks, h, 0, f] = one.astype(BF16).reshape(tile // 16, 16, 128)
            dk[:512] += two
            dv[:512] += three
            return inner

        dk[:512] = jnp.zeros((512, 128), F32)
        dv[:512] = jnp.zeros((512, 128), F32)
        lax.fori_loop(0, 512 // tile, rows, 0)
        gout[:, h, 1, f] = dk[:512].astype(BF16).reshape(32, 16, 128)
        gout[:, h, 2, f] = dv[:512].astype(BF16).reshape(32, 16, 128)
        return carry

    lax.fori_loop(0, 2, frame, 0)


def vmem():
    return pl.BlockSpec(memory_space=pltpu.VMEM)


def anywhere():
    return pl.BlockSpec(memory_space=pl.ANY)


def ring_scratch(width):
    return [
        pltpu.VMEM((8, 2, 96, width), BF16),
        pltpu.VMEM((2, 4, 2, 96, width), BF16),
        pltpu.VMEM((96, width), BF16),
    ]


def run_main(w, v, y, res, shift, scale, qkv, grad, sout, sqkv):
    dma = pltpu.SemaphoreType.DMA
    return pl.pallas_call(
        main_kernel,
        out_shape=(
            jax.ShapeDtypeStruct((3, 2, 32, 2, 16, 128), BF16),
            jax.ShapeDtypeStruct((128, 3072), BF16),
            jax.ShapeDtypeStruct((2, 3, 96, 128), F32),
            jax.ShapeDtypeStruct((2, 96, 128), F32),
        ),
        in_specs=[vmem(), vmem(), vmem(), anywhere(), vmem(), vmem()] + [anywhere()] * 4,
        out_specs=(vmem(),) * 4,
        scratch_shapes=[
            pltpu.VMEM((32, 96, 1024), BF16),
            pltpu.VMEM((8, 128, 3072), BF16),
            pltpu.VMEM((1024, 768), BF16),
            pltpu.VMEM((1024, 128), F32),
            pltpu.VMEM((1024, 128), F32),
            pltpu.VMEM((8, 128, 3072), BF16),
            pltpu.VMEM((4, 64, 3072), BF16),
            pltpu.VMEM((3, 2, 32, 3072), BF16),
            pltpu.VMEM((3, 2, 64, 3072), BF16),
            pltpu.VMEM((64, 3072), BF16),
            pltpu.VMEM((8, 4, 96, 768), BF16),
            *ring_scratch(768),
            pltpu.VMEM((8, 128, 3072), BF16),
            pltpu.VMEM((32, 32, 256), BF16),
            pltpu.VMEM((32, 32, 256), BF16),
            pltpu.VMEM((32, 2, 3, 2, 16, 128), BF16),
            pltpu.VMEM((8, 4, 96, 256), BF16),
            pltpu.VMEM((8, 2, 96, 256), BF16),
            pltpu.VMEM((8, 96, 256), BF16),
            pltpu.VMEM((8, 96, 256), BF16),
            dma((130,)),
            dma((130,)),
            dma((8, 2)),
            dma((8, 2)),
            dma((8, 2)),
            dma((8, 2)),
            dma((32,)),
            dma((32,)),
            dma((2, 32)),
            dma((2, 32)),
            pltpu.VMEM((3, 2, 1024, 128), BF16),
            pltpu.VMEM((2, 1024, 128), BF16),
            pltpu.VMEM((128, 3072), BF16),
            pltpu.VMEM((2, 1024, 128), BF16),
            pltpu.VMEM((3, 2, 2, 512, 128), BF16),
            dma((5,)),
        ],
        compiler_params=pltpu.CompilerParams(
            collective_id=0, has_side_effects=True, vmem_limit_bytes=63 << 20
        ),
        name="main",
    )(w, v, y, res, shift, scale, qkv, grad, sout, sqkv)


def local(
    y_rows, grad_res, shift, scale_mod, temporal_qkv, temporal_grad,
    spatial_qkv, spatial_out, w_temporal, w_spatial,
):
    grads, ig, wt, ws = run_main(
        jnp.transpose(w_temporal, (0, 2, 1, 3)),
        w_spatial,
        y_rows.reshape(128, 3072),
        grad_res.reshape(128, 3072),
        shift.reshape(1, 3072),
        scale_mod.reshape(1, 3072),
        temporal_qkv.reshape(3, 2, 1024, 128),
        temporal_grad.reshape(2, 1024, 128),
        spatial_out.reshape(2, 1024, 128),
        spatial_qkv,
    )
    by_heads = grads.reshape(3, 2, 64, 16, 128)
    wt = jnp.transpose(wt, (0, 2, 1, 3))
    return by_heads, ig.reshape(8, 16, 3072), wt, ws


def solution(mesh):
    placed = (
        P("seq", "pos", None),
        P("seq", "pos", None),
        P(),
        P(),
        P(None, "seq", None, "pos", None),
        P("seq", None, "pos", None),
        P(None, "seq", "pos", None, None),
        P("seq", None, "pos", None),
        P("seq", "pos", None, None),
        P("seq", "pos", None),
    )
    return jax.shard_map(
        local,
        mesh=mesh,
        in_specs=placed,
        out_specs=(
            P(None, "seq", None, "pos", None),
            P("seq", "pos", None),
            P("seq", "pos", None, None),
            P("seq", "pos", None),
        ),
        check_vma=False,
    )
```

```python
import jax
import jax.numpy as jnp
from jax import lax
from jax.experimental import pallas as pl
from jax.experimental.pallas import tpu as pltpu
from jax.sharding import PartitionSpec as P

MESH = pl.DeviceIdType.MESH
F32 = jnp.float32
BF16 = jnp.bfloat16
NT = (((1,), (1,)), ((), ()))
TN = (((0,), (0,)), ((), ()))
NN = (((1,), (0,)), ((), ()))
CUT, REST = 14 * 128, 10 * 128


def dot(a, b, dims=NN):
    return lax.dot_general(a, b, dims, preferred_element_type=F32)


class Place:
    def __init__(self):
        s, p = lax.axis_index("seq"), lax.axis_index("pos")
        self.yl, self.x = s // 4, s % 4
        self.z, self.yh, self.co = p // 4, (p // 2) % 2, p % 2

    def at(self, yl=None, x=None, z=None, yh=None, co=None):
        yl = self.yl if yl is None else yl
        x = self.x if x is None else x
        z = self.z if z is None else z
        yh = self.yh if yh is None else yh
        co = self.co if co is None else co
        return (yl * 4 + x, z * 4 + yh * 2 + co)

    def dx(self, k):
        return (self.x + k + 4) % 4

    def dz(self, k):
        return (self.z + k + 8) % 8

    def neighbours(self, seq, pos):
        found = []
        if seq:
            found += [self.at(x=self.dx(1)), self.at(x=self.dx(-1)), self.at(yl=1 - self.yl)]
        if pos:
            found += [
                self.at(z=self.dz(1)),
                self.at(z=self.dz(-1)),
                self.at(yh=1 - self.yh),
                self.at(co=1 - self.co),
            ]
        return found


def meet(devices):
    barrier = pltpu.get_barrier_semaphore()
    for device in devices:
        pl.semaphore_signal(barrier, inc=1, device_id=device, device_id_type=MESH)
    pl.semaphore_wait(barrier, len(devices))


class Net:
    def __init__(self, send_sem, recv_sem):
        self.send_sem, self.recv_sem, self.count, self.open = send_sem, recv_sem, 0, []

    def send(self, source, target, device):
        i = self.count
        self.count += 1
        copy = pltpu.make_async_remote_copy(
            src_ref=source,
            dst_ref=target,
            send_sem=self.send_sem.at[i],
            recv_sem=self.recv_sem.at[i],
            device_id=device,
            device_id_type=MESH,
        )
        copy.start()
        self.open.append(copy)
        return copy

    def finish(self):
        for copy in self.open:
            copy.wait_send()
        self.open = []


def add_into(target, terms, rows, tile=16):
    def body(i, carry):
        at = pl.ds(pl.multiple_of(i * tile, tile), tile)
        total = target[at, :].astype(F32)
        for term in terms:
            total += term[at, :].astype(F32)
        target[at, :] = total.astype(BF16)
        return carry

    lax.fori_loop(0, rows // tile, body, 0)


def gather_pos(net, me, full):
    def slot(z, r, co):
        return full.at[z * 4 + ((me.yh + r) % 2) * 2 + co]

    up, down = me.at(z=me.dz(1)), me.at(z=me.dz(-1))
    other = me.at(co=1 - me.co)
    mine = slot(me.z, 0, me.co)
    cross = net.send(mine, mine, me.at(yh=1 - me.yh))
    plus = [net.send(mine, mine, up)]
    minus = [net.send(mine, mine, down)]
    cores = [net.send(mine, mine, other)]
    yield
    cross.wait_recv()
    near = slot(me.z, 1, me.co)
    plus.append(net.send(near, near, up))
    minus.append(net.send(near, near, down))
    cores.append(net.send(near, near, other))
    yield
    for k in range(1, 5):
        next_plus, next_minus = [], []
        for r in range(2):
            if k < 4 or r == 0:
                plus[r].wait_recv()
                block = slot(me.dz(-k), r, me.co)
                if k < 3 or (k == 3 and r == 0):
                    next_plus.append(net.send(block, block, up))
                else:
                    next_plus.append(None)
                cores.append(net.send(block, block, other))
            if k < 4 or r == 1:
                minus[r].wait_recv()
                block = slot(me.dz(k), r, me.co)
                if k < 3 or (k == 3 and r == 1):
                    next_minus.append(net.send(block, block, down))
                else:
                    next_minus.append(None)
                cores.append(net.send(block, block, other))
            if k < 4:
                yield
        plus, minus = next_plus, next_minus
    yield
    for copy in cores:
        copy.wait_recv()


def gather_seq(net, me, full, done):
    def part(yl, x, first, width):
        return full.at[yl * 4 + x, :, pl.ds(first, width)]

    yl, x, far = me.yl, me.x, 1 - me.yl
    left, right, xo = me.dx(-1), me.dx(1), me.dx(2)
    to_r, to_l, to_y = me.at(x=right), me.at(x=left), me.at(yl=far)

    def push(block, device):
        return net.send(block, block, device)

    def low(yl, x):
        return part(yl, x, 0, CUT)

    def high(yl, x):
        return part(yl, x, CUT, REST)

    y0, y1 = push(low(yl, x), to_y), push(high(yl, x), to_y)
    r1, l1 = push(high(yl, x), to_r), push(high(yl, x), to_l)
    r0, l0 = push(low(yl, x), to_r), push(low(yl, x), to_l)
    done((yl, x))
    yield
    r1.wait_recv()
    rc = push(part(yl, left, CUT, REST // 2), to_r)
    yr = push(high(yl, left), to_y)
    l1.wait_recv()
    ld = push(part(yl, right, CUT + REST // 2, REST // 2), to_l)
    yq = push(high(yl, right), to_y)
    yield
    y0.wait_recv()
    rf, lf = push(low(far, x), to_r), push(low(far, x), to_l)
    yield
    r0.wait_recv()
    ra = push(part(yl, left, 0, CUT // 2), to_r)
    l0.wait_recv()
    lb = push(part(yl, right, CUT // 2, CUT // 2), to_l)
    y1.wait_recv()
    done((far, x))
    done((yl, left))
    done((yl, right))
    yield
    rc.wait_recv()
    ld.wait_recv()
    yo = push(high(yl, xo), to_y)
    yield
    rf.wait_recv()
    re = push(part(far, left, 0, CUT // 2), to_r)
    lf.wait_recv()
    lg = push(part(far, right, CUT // 2, CUT // 2), to_l)
    yr.wait_recv()
    yq.wait_recv()
    done((far, left))
    done((far, right))
    yield
    ra.wait_recv()
    lb.wait_recv()
    done((yl, xo))
    yield
    re.wait_recv()
    lg.wait_recv()
    yo.wait_recv()
    done((far, xo))


def reduce_x(net, me, block, width, quarter, half):
    left, right, xo = me.dx(-1), me.dx(1), me.dx(2)
    to_r, to_l = me.at(x=right), me.at(x=left)
    one, two = pl.ds(0, width // 2), pl.ds(width // 2, width // 2)
    whole = pl.ds(0, width)
    near = [quarter.at[n, :, one] for n in range(2)]
    sums = [half.at[n, :, whole] for n in range(2)]
    a = net.send(block(xo).at[:, one], near[0], to_r)
    b = net.send(block(xo).at[:, two], near[1], to_l)
    yield
    a.wait_recv()
    add_into(block(right).at[:, one], [near[0]], 128)
    c = net.send(block(right), sums[0], to_r)
    b.wait_recv()
    add_into(block(left).at[:, two], [near[1]], 128)
    d = net.send(block(left), sums[1], to_l)
    yield
    c.wait_recv()
    d.wait_recv()
    add_into(block(me.x), sums, 128)


def reduce_pos_ring(net, me, part, core_recv, core_copies, ring, across, out):
    up, down = me.at(z=me.dz(1)), me.at(z=me.dz(-1))

    def slot(z, r):
        return part.at[z, ((me.yh + r) % 2) * 2 + me.co]

    def merge(z, k):
        core_copies[k].wait_recv()
        for r in range(2):
            add_into(slot(z, r), [core_recv.at[z, (me.yh + r) % 2]], 96)

    merge(me.dz(4), 0)
    plus = [net.send(slot(me.dz(4), 0), ring.at[0, 0, 0], up), None]
    minus = [None, net.send(slot(me.dz(4), 1), ring.at[1, 0, 1], down)]
    merge(me.dz(3), 1)
    merge(me.dz(-3), 2)
    yield
    for k in range(1, 4):
        next_plus, next_minus = [], []
        for r in range(2):
            at = slot(me.dz(4 - k), r)
            if plus[r] is not None:
                plus[r].wait_recv()
                add_into(at, [ring.at[0, k - 1, r]], 96)
            next_plus.append(net.send(at, ring.at[0, k, r], up))
            at = slot(me.dz(k - 4), r)
            if minus[r] is not None:
                minus[r].wait_recv()
                add_into(at, [ring.at[1, k - 1, r]], 96)
            next_minus.append(net.send(at, ring.at[1, k, r], down))
        plus, minus = next_plus, next_minus
        if k < 3:
            merge(me.dz(3 - k), 2 * k + 1)
            merge(me.dz(k - 3), 2 * k + 2)
        else:
            merge(me.z, 7)
        yield
    for r in (1, 0):
        plus[r].wait_recv()
        minus[r].wait_recv()
        add_into(slot(me.z, r), [ring.at[0, 3, r], ring.at[1, 3, r]], 96)
        if r == 1:
            swap = net.send(slot(me.z, 1), across, me.at(yh=1 - me.yh))
    yield
    swap.wait_recv()
    out(slot(me.z, 0)[...].astype(F32) + across[...].astype(F32))


def reduce_pos_direct(net, me, part, core_recv, core_copies, from_yh, from_z, out):
    def slot(z, r):
        return part.at[z, ((me.yh + r) % 2) * 2 + me.co]

    for i in range(8):
        core_copies[i].wait_recv()

    def merge(z, carry):
        for r in range(2):
            add_into(slot(z, r), [core_recv.at[z, (me.yh + r) % 2]], 96)
        return carry

    lax.fori_loop(0, 8, merge, 0)
    swap = net.send(
        part.at[:, (1 - me.yh) * 2 + me.co], from_yh, me.at(yh=1 - me.yh)
    )
    yield
    swap.wait_recv()

    def join(z, carry):
        add_into(slot(z, 0), [from_yh.at[z]], 96)
        return carry

    lax.fori_loop(0, 8, join, 0)
    copies = [
        net.send(slot(me.dz(k), 0), from_z.at[me.z], me.at(z=me.dz(k)))
        for k in (4, 3, 5, 2, 6, 1, 7)
    ]
    yield
    for copy in copies:
        copy.wait_recv()
    total = slot(me.z, 0)[...].astype(F32)
    for k in range(1, 8):
        total += from_z[me.dz(k)].astype(F32)
    out(total)


def z_order(i):
    return 4 + (1 - 2 * (i % 2)) * ((i + 1) // 2)


def core_copy(me, part, core_recv, send_sem, recv_sem, zt, i):
    copies = []
    for yh in range(2):
        copies.append(
            pltpu.make_async_remote_copy(
                src_ref=part.at[zt, yh * 2 + 1 - me.co],
                dst_ref=core_recv.at[zt, yh],
                send_sem=send_sem.at[i, yh],
                recv_sem=recv_sem.at[i, yh],
                device_id=me.at(co=1 - me.co),
                device_id_type=MESH,
            )
        )
    return copies


class Pair:
    def __init__(self, copies):
        self.copies = copies

    def wait_recv(self):
        for copy in self.copies:
            copy.wait_recv()


def core_copies_of(me, part, core_recv, send_sem, recv_sem):
    return [
        Pair(core_copy(me, part, core_recv, send_sem, recv_sem, me.dz(z_order(i) - 8), i))
        for i in range(8)
    ]


def weight_partial(me, rows_ref, right, part, core_recv, send_sem, recv_sem):
    def body(i, carry):
        zt = (me.z + z_order(i)) % 8
        at = pl.ds(pl.multiple_of(zt * 384, 128), 384)
        left = rows_ref[:, :, at].reshape(1024, 384)
        result = dot(left, right(), TN).astype(BF16)
        part[zt] = result.reshape(4, 96, result.shape[-1])
        for copy in core_copy(me, part, core_recv, send_sem, recv_sem, zt, i):
            copy.start()
        return carry

    lax.fori_loop(0, 8, body, 0)


def attention_rows(q, k, v, g, mask):
    factor = 128**-0.5
    s = dot(q, k, NT) * factor
    if mask is not None:
        s = jnp.where(mask, s, -1e30)
    e = jnp.exp(s - jnp.max(s, axis=-1, keepdims=True))
    p = e * (1.0 / jnp.sum(e, axis=-1, keepdims=True))
    dp = dot(g, v, NT)
    inner = jnp.sum(p * dp, axis=-1, keepdims=True)
    ds = (p * (dp - inner) * factor).astype(BF16)
    return dot(ds, k), dot(ds, q, TN), dot(p.astype(BF16), g, TN)


def temporal(h, qkv, grad, dk, dv, out):
    tile = 128
    rows = lax.broadcasted_iota(jnp.int32, (tile, 1024), 0)
    cols = lax.broadcasted_iota(jnp.int32, (tile, 1024), 1)
    mask = (rows % 16) == (cols % 16)

    def body(t, carry):
        at = pl.ds(pl.multiple_of(t * tile, tile), tile)
        one, two, three = attention_rows(
            qkv[0, h, at, :], qkv[1, h], qkv[2, h], grad[h, at, :], mask
        )
        out[at, pl.ds(h * 384, 128)] = one.astype(BF16)
        dk[...] += two
        dv[...] += three
        return carry

    dk[...] = jnp.zeros_like(dk)
    dv[...] = jnp.zeros_like(dv)
    lax.fori_loop(0, 1024 // tile, body, 0)
    out[:, pl.ds(h * 384 + 128, 128)] = dk[...].astype(BF16)
    out[:, pl.ds(h * 384 + 256, 128)] = dv[...].astype(BF16)


def unit_of(y):
    values = y.astype(F32)
    center = values - jnp.mean(values, axis=-1, keepdims=True)
    inverse = lax.rsqrt(jnp.mean(center * center, axis=-1, keepdims=True) + 1e-06)
    return center * inverse, inverse


def main_kernel(
    w_ref, v_ref, y_ref, res_ref, shift_ref, scale_ref, qkv_ref, grad_ref, sout_ref, sqkv_ref,
    out_ref, ig_ref, wt_ref, ws_ref,
    wf, nf, dq, dk, dv, part, from_y, quarter, half, last_y,
    wpart, core_recv, ring, across, igf,
    gso, byf, gout, wspart, core_recv_s, from_yh, from_z,
    send_sem, recv_sem, core_send, core_recv_sem, core_send_s, core_recv_sem_s,
    gso_send, gso_recv, out_send, out_recv,
    qkv, grad, res, sout, sqkv, local_sem,
):
    me = Place()
    net = Net(send_sem, recv_sem)
    s_own = me.yl * 4 + me.x
    p_own = lax.axis_index("pos")
    far = 1 - me.yl
    local_copies = [
        pltpu.make_async_copy(source, target, local_sem.at[i])
        for i, (source, target) in enumerate(
            [(qkv_ref, qkv), (grad_ref, grad), (res_ref, res), (sout_ref, sout), (sqkv_ref, sqkv)]
        )
    ]
    for copy in local_copies:
        copy.start()
    meet(me.neighbours(True, True))

    def norm_tile(i, carry):
        at = pl.ds(pl.multiple_of(i * 16, 16), 16)
        unit, _ = unit_of(y_ref[at, :])
        nf[s_own, at, :] = (unit * (1.0 + scale_ref[...]) + shift_ref[...]).astype(BF16)
        return carry

    for h in range(2):
        for c in range(3):
            wf[p_own, :, pl.ds((h * 3 + c) * 128, 128)] = w_ref[h, c]
        wf[p_own, :, pl.ds(768 + h * 128, 128)] = v_ref[h]
    first = gather_pos(net, me, wf)
    second = gather_seq(net, me, nf, lambda at: None)
    next(first)
    lax.fori_loop(0, 8, norm_tile, 0)
    next(second)
    for copy in local_copies[:2]:
        copy.wait()
    temporal(0, qkv, grad, dk, dv, dq)
    next(first)
    next(first)
    next(second)
    next(second)
    temporal(1, qkv, grad, dk, dv, dq)
    next(first)
    next(first)
    next(second)
    next(first)
    next(second)
    next(first)
    next(first)
    next(second)
    for _ in first:
        pass

    def partial(x):
        lhs = jnp.concatenate(
            [dq[pl.ds(pl.multiple_of((yl * 4 + x) * 128, 128), 128), :] for yl in range(2)], axis=0
        )

        def body(z, carry):
            w = wf[pl.ds(z * 4, 4), :, pl.ds(0, 768)].reshape(384, 768)
            result = dot(lhs, w, NT).astype(BF16)
            at = pl.ds(pl.multiple_of(z * 384, 128), 384)
            part[x, :, at] = result[:128]
            part[4 + x, :, at] = result[128:]
            return carry

        lax.fori_loop(0, 8, body, 0)

    def low(yl):
        return lambda x: part.at[yl * 4 + x, :, pl.ds(0, CUT)]

    def high(x):
        return part.at[me.yl * 4 + x, :, pl.ds(CUT, REST)]

    def to_partner(x):
        return net.send(part.at[far * 4 + x, :, pl.ds(CUT, REST)], from_y.at[x], me.at(yl=far))

    def take(i):
        swaps[i].wait_recv()
        add_into(high(order[i]), [from_y.at[order[i]]], 128)

    swaps = {}
    order = [me.dx(2), me.dx(1), me.dx(-1), me.x]
    red_far = reduce_x(net, me, low(far), CUT, quarter.at[0], half.at[0])
    red_own = reduce_x(net, me, low(me.yl), CUT, quarter.at[1], half.at[1])
    red_two = reduce_x(net, me, high, REST, quarter.at[2], half.at[2])
    partial(order[0])
    next(red_far)
    swaps[0] = to_partner(order[0])
    next(red_own)
    for i in range(1, 4):
        partial(order[i])
        swaps[i] = to_partner(order[i])
    next(red_far)
    take(0)
    next(red_two)
    next(red_own)

    for _ in second:
        pass
    weight_partial(me, nf, lambda: dq[...], wpart, core_recv, core_send, core_recv_sem)
    core = core_copies_of(me, wpart, core_recv, core_send, core_recv_sem)

    def wt_total(value):
        for h in range(2):
            for c in range(3):
                wt_ref[h, c] = value[:, (h * 3 + c) * 128 : (h * 3 + c + 1) * 128]

    def ws_total(value):
        for h in range(2):
            ws_ref[h] = value[:, h * 128 : (h + 1) * 128]

    wt_steps = reduce_pos_ring(net, me, wpart, core_recv, core, ring, across, wt_total)

    take(1)
    take(2)
    next(wt_steps)
    for _ in red_far:
        pass
    swap = net.send(part.at[far * 4 + me.x, :, pl.ds(0, CUT)], last_y, me.at(yl=far))
    next(red_two)
    next(wt_steps)
    take(3)
    for _ in red_own:
        pass
    for _ in red_two:
        pass
    swap.wait_recv()

    for copy in local_copies[2:]:
        copy.wait()

    def back_tile(i, carry):
        at = pl.ds(pl.multiple_of(i * 16, 16), 16)
        total = part[s_own, at, :].astype(F32)
        more = total[:, :CUT] + last_y[at, :].astype(F32)
        total = jnp.concatenate([more, total[:, CUT:]], axis=1)
        unit, inverse = unit_of(y_ref[at, :])
        scaled = total * (1.0 + scale_ref[...])
        one = jnp.mean(scaled, axis=-1, keepdims=True)
        two = jnp.mean(scaled * unit, axis=-1, keepdims=True)
        result = res[at, :].astype(F32) + inverse * (scaled - one - unit * two)
        result = result.astype(BF16)
        igf[s_own, at, :] = result
        ig_ref[at, :] = result
        return carry

    lax.fori_loop(0, 8, back_tile, 0)

    def gso_copy(p_to, p_from):
        return pltpu.make_async_remote_copy(
            src_ref=gso.at[p_to],
            dst_ref=byf.at[p_from],
            send_sem=gso_send.at[p_to],
            recv_sem=gso_recv.at[p_from],
            device_id=(s_own, p_to),
            device_id_type=MESH,
        )

    def project(blocks):
        def body(i, carry):
            s = blocks[0]
            for n in range(1, len(blocks)):
                s = jnp.where(i == n, blocks[n], s)
            w = wf[:, :, pl.ds(768, 256)].reshape(3072, 256)
            result = dot(igf[s], w).astype(BF16).reshape(4, 32, 256)
            gso[pl.ds(s * 4, 4)] = result
            for n in range(4):
                p_to = s * 4 + n

                @pl.when(p_to == p_own)
                def _():
                    byf[p_to] = result[n]

                @pl.when(p_to != p_own)
                def _():
                    gso_copy(p_to, p_own).start()

            return carry

        lax.fori_loop(0, len(blocks), body, 0)

    def others(body):
        def step(i, carry):
            body((p_own + 16 + (1 - 2 * (i % 2)) * ((i + 1) // 2)) % 32)
            return carry

        lax.fori_loop(0, 31, step, 0)

    def out_copy(h, p_to, p_from):
        return pltpu.make_async_remote_copy(
            src_ref=gout.at[p_to, h],
            dst_ref=out_ref.at[:, h, p_from],
            send_sem=out_send.at[h, p_to],
            recv_sem=out_recv.at[h, p_from],
            device_id=(s_own, p_to),
            device_id_type=MESH,
        )

    def attend(h):
        if h == 0:
            others(lambda p: gso_copy(p_own, p).wait_recv())
        spatial(h, sqkv, byf, dk, dv, gout)
        out_ref[:, h, p_own] = gout[p_own, h]
        others(lambda p: out_copy(h, p, p_own).start())

    pending = []

    def come():
        blocks = list(pending)
        pending.clear()
        project(blocks)
        return blocks

    last = gather_seq(net, me, igf, lambda at: pending.append(at[0] * 4 + at[1]))
    next(last)
    come()
    next(wt_steps)
    next(last)
    next(last)
    next(last)
    come()
    next(last)
    next(wt_steps)
    next(last)
    come()
    for _ in wt_steps:
        pass
    next(last)
    come()
    for _ in last:
        pass
    come()

    weight_partial(
        me,
        igf,
        lambda: jnp.concatenate([sout[0], sout[1]], axis=1),
        wspart,
        core_recv_s,
        core_send_s,
        core_recv_sem_s,
    )
    core_s = core_copies_of(me, wspart, core_recv_s, core_send_s, core_recv_sem_s)
    ws_steps = reduce_pos_direct(
        net, me, wspart, core_recv_s, core_s, from_yh, from_z, ws_total
    )
    next(ws_steps)
    for h in range(2):
        attend(h)
        next(ws_steps, None)
    for _ in ws_steps:
        pass
    for h in range(2):
        others(lambda p: out_copy(h, p_own, p).wait_recv())
    for h in range(2):
        others(lambda p: out_copy(h, p, p_own).wait_send())
    others(lambda p: gso_copy(p, p_own).wait_send())
    for pair in core + core_s:
        for copy in pair.copies:
            copy.wait_send()
    net.finish()


def spatial(h, qkv, byf, dk, dv, gout):
    tile = 256

    def frame(f, carry):
        def rows(t, inner):
            at = pl.ds(pl.multiple_of(t * tile, tile), tile)
            blocks = pl.ds(t * (tile // 16), tile // 16)
            g = byf[blocks, pl.ds(f * 16, 16), pl.ds(h * 128, 128)].reshape(tile, 128)
            one, two, three = attention_rows(
                qkv[0, h, f, at, :], qkv[1, h, f], qkv[2, h, f], g, None
            )
            gout[blocks, h, 0, f] = one.astype(BF16).reshape(tile // 16, 16, 128)
            dk[:512] += two
            dv[:512] += three
            return inner

        dk[:512] = jnp.zeros((512, 128), F32)
        dv[:512] = jnp.zeros((512, 128), F32)
        lax.fori_loop(0, 512 // tile, rows, 0)
        gout[:, h, 1, f] = dk[:512].astype(BF16).reshape(32, 16, 128)
        gout[:, h, 2, f] = dv[:512].astype(BF16).reshape(32, 16, 128)
        return carry

    lax.fori_loop(0, 2, frame, 0)


def vmem():
    return pl.BlockSpec(memory_space=pltpu.VMEM)


def anywhere():
    return pl.BlockSpec(memory_space=pl.ANY)


def ring_scratch(width):
    return [
        pltpu.VMEM((8, 2, 96, width), BF16),
        pltpu.VMEM((2, 4, 2, 96, width), BF16),
        pltpu.VMEM((96, width), BF16),
    ]


def run_main(w, v, y, res, shift, scale, qkv, grad, sout, sqkv):
    dma = pltpu.SemaphoreType.DMA
    return pl.pallas_call(
        main_kernel,
        out_shape=(
            jax.ShapeDtypeStruct((3, 2, 32, 2, 16, 128), BF16),
            jax.ShapeDtypeStruct((128, 3072), BF16),
            jax.ShapeDtypeStruct((2, 3, 96, 128), F32),
            jax.ShapeDtypeStruct((2, 96, 128), F32),
        ),
        in_specs=[vmem(), vmem(), vmem(), anywhere(), vmem(), vmem()] + [anywhere()] * 4,
        out_specs=(vmem(),) * 4,
        scratch_shapes=[
            pltpu.VMEM((32, 96, 1024), BF16),
            pltpu.VMEM((8, 128, 3072), BF16),
            pltpu.VMEM((1024, 768), BF16),
            pltpu.VMEM((1024, 128), F32),
            pltpu.VMEM((1024, 128), F32),
            pltpu.VMEM((8, 128, 3072), BF16),
            pltpu.VMEM((4, 128, REST), BF16),
            pltpu.VMEM((3, 2, 128, CUT // 2), BF16),
            pltpu.VMEM((3, 2, 128, CUT), BF16),
            pltpu.VMEM((128, CUT), BF16),
            pltpu.VMEM((8, 4, 96, 768), BF16),
            *ring_scratch(768),
            pltpu.VMEM((8, 128, 3072), BF16),
            pltpu.VMEM((32, 32, 256), BF16),
            pltpu.VMEM((32, 32, 256), BF16),
            pltpu.VMEM((32, 2, 3, 2, 16, 128), BF16),
            pltpu.VMEM((8, 4, 96, 256), BF16),
            pltpu.VMEM((8, 2, 96, 256), BF16),
            pltpu.VMEM((8, 96, 256), BF16),
            pltpu.VMEM((8, 96, 256), BF16),
            dma((130,)),
            dma((130,)),
            dma((8, 2)),
            dma((8, 2)),
            dma((8, 2)),
            dma((8, 2)),
            dma((32,)),
            dma((32,)),
            dma((2, 32)),
            dma((2, 32)),
            pltpu.VMEM((3, 2, 1024, 128), BF16),
            pltpu.VMEM((2, 1024, 128), BF16),
            pltpu.VMEM((128, 3072), BF16),
            pltpu.VMEM((2, 1024, 128), BF16),
            pltpu.VMEM((3, 2, 2, 512, 128), BF16),
            dma((5,)),
        ],
        compiler_params=pltpu.CompilerParams(
            collective_id=0, has_side_effects=True, vmem_limit_bytes=63 << 20
        ),
        name="main",
    )(w, v, y, res, shift, scale, qkv, grad, sout, sqkv)


def local(
    y_rows, grad_res, shift, scale_mod, temporal_qkv, temporal_grad,
    spatial_qkv, spatial_out, w_temporal, w_spatial,
):
    grads, ig, wt, ws = run_main(
        jnp.transpose(w_temporal, (0, 2, 1, 3)),
        w_spatial,
        y_rows.reshape(128, 3072),
        grad_res.reshape(128, 3072),
        shift.reshape(1, 3072),
        scale_mod.reshape(1, 3072),
        temporal_qkv.reshape(3, 2, 1024, 128),
        temporal_grad.reshape(2, 1024, 128),
        spatial_out.reshape(2, 1024, 128),
        spatial_qkv,
    )
    by_heads = grads.reshape(3, 2, 64, 16, 128)
    wt = jnp.transpose(wt, (0, 2, 1, 3))
    return by_heads, ig.reshape(8, 16, 3072), wt, ws


def solution(mesh):
    placed = (
        P("seq", "pos", None),
        P("seq", "pos", None),
        P(),
        P(),
        P(None, "seq", None, "pos", None),
        P("seq", None, "pos", None),
        P(None, "seq", "pos", None, None),
        P("seq", None, "pos", None),
        P("seq", "pos", None, None),
        P("seq", "pos", None),
    )
    return jax.shard_map(
        local,
        mesh=mesh,
        in_specs=placed,
        out_specs=(
            P(None, "seq", None, "pos", None),
            P("seq", "pos", None),
            P("seq", "pos", None, None),
            P("seq", "pos", None),
        ),
        check_vma=False,
    )
```

```python
import jax
import jax.numpy as jnp
from jax import lax
from jax.experimental import pallas as pl
from jax.experimental.pallas import tpu as pltpu
from jax.sharding import PartitionSpec as P

MESH = pl.DeviceIdType.MESH
F32 = jnp.float32
BF16 = jnp.bfloat16
NT = (((1,), (1,)), ((), ()))
TN = (((0,), (0,)), ((), ()))
NN = (((1,), (0,)), ((), ()))
CUT, REST = 14 * 128, 10 * 128


def dot(a, b, dims=NN):
    return lax.dot_general(a, b, dims, preferred_element_type=F32)


class Place:
    def __init__(self):
        s, p = lax.axis_index("seq"), lax.axis_index("pos")
        self.yl, self.x = s // 4, s % 4
        self.z, self.yh, self.co = p // 4, (p // 2) % 2, p % 2

    def at(self, yl=None, x=None, z=None, yh=None, co=None):
        yl = self.yl if yl is None else yl
        x = self.x if x is None else x
        z = self.z if z is None else z
        yh = self.yh if yh is None else yh
        co = self.co if co is None else co
        return (yl * 4 + x, z * 4 + yh * 2 + co)

    def dx(self, k):
        return (self.x + k + 4) % 4

    def dz(self, k):
        return (self.z + k + 8) % 8

    def neighbours(self, seq, pos):
        found = []
        if seq:
            found += [self.at(x=self.dx(1)), self.at(x=self.dx(-1)), self.at(yl=1 - self.yl)]
        if pos:
            found += [
                self.at(z=self.dz(1)),
                self.at(z=self.dz(-1)),
                self.at(yh=1 - self.yh),
                self.at(co=1 - self.co),
            ]
        return found


def meet(devices):
    barrier = pltpu.get_barrier_semaphore()
    for device in devices:
        pl.semaphore_signal(barrier, inc=1, device_id=device, device_id_type=MESH)
    pl.semaphore_wait(barrier, len(devices))


class Net:
    def __init__(self, send_sem, recv_sem):
        self.send_sem, self.recv_sem, self.count, self.open = send_sem, recv_sem, 0, []

    def send(self, source, target, device):
        i = self.count
        self.count += 1
        copy = pltpu.make_async_remote_copy(
            src_ref=source,
            dst_ref=target,
            send_sem=self.send_sem.at[i],
            recv_sem=self.recv_sem.at[i],
            device_id=device,
            device_id_type=MESH,
        )
        copy.start()
        self.open.append(copy)
        return copy

    def finish(self):
        for copy in self.open:
            copy.wait_send()
        self.open = []


def add_into(target, terms, rows, tile=16):
    def body(i, carry):
        at = pl.ds(pl.multiple_of(i * tile, tile), tile)
        total = target[at, :].astype(F32)
        for term in terms:
            total += term[at, :].astype(F32)
        target[at, :] = total.astype(BF16)
        return carry

    lax.fori_loop(0, rows // tile, body, 0)


def gather_pos(net, me, full):
    def slot(z, r, co):
        return full.at[z * 4 + ((me.yh + r) % 2) * 2 + co]

    up, down = me.at(z=me.dz(1)), me.at(z=me.dz(-1))
    other = me.at(co=1 - me.co)
    mine = slot(me.z, 0, me.co)
    cross = net.send(mine, mine, me.at(yh=1 - me.yh))
    plus = [net.send(mine, mine, up)]
    minus = [net.send(mine, mine, down)]
    cores = [net.send(mine, mine, other)]
    yield
    cross.wait_recv()
    near = slot(me.z, 1, me.co)
    plus.append(net.send(near, near, up))
    minus.append(net.send(near, near, down))
    cores.append(net.send(near, near, other))
    yield
    for k in range(1, 5):
        next_plus, next_minus = [], []
        for r in range(2):
            if k < 4 or r == 0:
                plus[r].wait_recv()
                block = slot(me.dz(-k), r, me.co)
                if k < 3 or (k == 3 and r == 0):
                    next_plus.append(net.send(block, block, up))
                else:
                    next_plus.append(None)
                cores.append(net.send(block, block, other))
            if k < 4 or r == 1:
                minus[r].wait_recv()
                block = slot(me.dz(k), r, me.co)
                if k < 3 or (k == 3 and r == 1):
                    next_minus.append(net.send(block, block, down))
                else:
                    next_minus.append(None)
                cores.append(net.send(block, block, other))
            if k < 4:
                yield
        plus, minus = next_plus, next_minus
    yield
    for copy in cores:
        copy.wait_recv()


def gather_seq(net, me, full, done):
    def part(yl, x, first, width):
        return full.at[yl * 4 + x, :, pl.ds(first, width)]

    yl, x, far = me.yl, me.x, 1 - me.yl
    left, right, xo = me.dx(-1), me.dx(1), me.dx(2)
    to_r, to_l, to_y = me.at(x=right), me.at(x=left), me.at(yl=far)

    def push(block, device):
        return net.send(block, block, device)

    def low(yl, x):
        return part(yl, x, 0, CUT)

    def high(yl, x):
        return part(yl, x, CUT, REST)

    y0, y1 = push(low(yl, x), to_y), push(high(yl, x), to_y)
    r1, l1 = push(high(yl, x), to_r), push(high(yl, x), to_l)
    r0, l0 = push(low(yl, x), to_r), push(low(yl, x), to_l)
    done((yl, x))
    yield
    r1.wait_recv()
    rc = push(part(yl, left, CUT, REST // 2), to_r)
    yr = push(high(yl, left), to_y)
    l1.wait_recv()
    ld = push(part(yl, right, CUT + REST // 2, REST // 2), to_l)
    yq = push(high(yl, right), to_y)
    yield
    y0.wait_recv()
    rf, lf = push(low(far, x), to_r), push(low(far, x), to_l)
    yield
    r0.wait_recv()
    ra = push(part(yl, left, 0, CUT // 2), to_r)
    l0.wait_recv()
    lb = push(part(yl, right, CUT // 2, CUT // 2), to_l)
    y1.wait_recv()
    done((far, x))
    done((yl, left))
    done((yl, right))
    yield
    rc.wait_recv()
    ld.wait_recv()
    yo = push(high(yl, xo), to_y)
    yield
    rf.wait_recv()
    re = push(part(far, left, 0, CUT // 2), to_r)
    lf.wait_recv()
    lg = push(part(far, right, CUT // 2, CUT // 2), to_l)
    yr.wait_recv()
    yq.wait_recv()
    done((far, left))
    done((far, right))
    yield
    ra.wait_recv()
    lb.wait_recv()
    done((yl, xo))
    yield
    re.wait_recv()
    lg.wait_recv()
    yo.wait_recv()
    done((far, xo))


def reduce_x(net, me, block, width, quarter, half):
    left, right, xo = me.dx(-1), me.dx(1), me.dx(2)
    to_r, to_l = me.at(x=right), me.at(x=left)
    one, two = pl.ds(0, width // 2), pl.ds(width // 2, width // 2)
    whole = pl.ds(0, width)
    near = [quarter.at[n, :, one] for n in range(2)]
    sums = [half.at[n, :, whole] for n in range(2)]
    a = net.send(block(xo).at[:, one], near[0], to_r)
    b = net.send(block(xo).at[:, two], near[1], to_l)
    yield
    a.wait_recv()
    add_into(block(right).at[:, one], [near[0]], 128)
    c = net.send(block(right), sums[0], to_r)
    b.wait_recv()
    add_into(block(left).at[:, two], [near[1]], 128)
    d = net.send(block(left), sums[1], to_l)
    yield
    c.wait_recv()
    d.wait_recv()
    add_into(block(me.x), sums, 128)


def reduce_pos_ring(net, me, part, core_recv, core_copies, ring, across, out):
    up, down = me.at(z=me.dz(1)), me.at(z=me.dz(-1))

    def slot(z, r):
        return part.at[z, ((me.yh + r) % 2) * 2 + me.co]

    def merge(z, k):
        core_copies[k].wait_recv()
        for r in range(2):
            add_into(slot(z, r), [core_recv.at[z, (me.yh + r) % 2]], 96)

    merge(me.dz(4), 0)
    plus = [net.send(slot(me.dz(4), 0), ring.at[0, 0, 0], up), None]
    minus = [None, net.send(slot(me.dz(4), 1), ring.at[1, 0, 1], down)]
    merge(me.dz(3), 1)
    merge(me.dz(-3), 2)
    yield
    for k in range(1, 4):
        next_plus, next_minus = [], []
        for r in range(2):
            at = slot(me.dz(4 - k), r)
            if plus[r] is not None:
                plus[r].wait_recv()
                add_into(at, [ring.at[0, k - 1, r]], 96)
            next_plus.append(net.send(at, ring.at[0, k, r], up))
            at = slot(me.dz(k - 4), r)
            if minus[r] is not None:
                minus[r].wait_recv()
                add_into(at, [ring.at[1, k - 1, r]], 96)
            next_minus.append(net.send(at, ring.at[1, k, r], down))
        plus, minus = next_plus, next_minus
        if k < 3:
            merge(me.dz(3 - k), 2 * k + 1)
            merge(me.dz(k - 3), 2 * k + 2)
        else:
            merge(me.z, 7)
        yield
    for r in (1, 0):
        plus[r].wait_recv()
        minus[r].wait_recv()
        add_into(slot(me.z, r), [ring.at[0, 3, r], ring.at[1, 3, r]], 96)
        if r == 1:
            swap = net.send(slot(me.z, 1), across, me.at(yh=1 - me.yh))
    yield
    swap.wait_recv()
    out(slot(me.z, 0)[...].astype(F32) + across[...].astype(F32))


def reduce_pos_direct(net, me, part, core_recv, core_copies, from_yh, from_z, out):
    def slot(z, r):
        return part.at[z, ((me.yh + r) % 2) * 2 + me.co]

    for i in range(8):
        core_copies[i].wait_recv()

    def merge(z, carry):
        for r in range(2):
            add_into(slot(z, r), [core_recv.at[z, (me.yh + r) % 2]], 96)
        return carry

    lax.fori_loop(0, 8, merge, 0)
    swap = net.send(
        part.at[:, (1 - me.yh) * 2 + me.co], from_yh, me.at(yh=1 - me.yh)
    )
    yield
    swap.wait_recv()

    def join(z, carry):
        add_into(slot(z, 0), [from_yh.at[z]], 96)
        return carry

    lax.fori_loop(0, 8, join, 0)
    copies = [
        net.send(slot(me.dz(k), 0), from_z.at[me.z], me.at(z=me.dz(k)))
        for k in (4, 3, 5, 2, 6, 1, 7)
    ]
    yield
    for copy in copies:
        copy.wait_recv()
    total = slot(me.z, 0)[...].astype(F32)
    for k in range(1, 8):
        total += from_z[me.dz(k)].astype(F32)
    out(total)


def z_order(i):
    return 4 + (1 - 2 * (i % 2)) * ((i + 1) // 2)


def core_copy(me, part, core_recv, send_sem, recv_sem, zt, i):
    copies = []
    for yh in range(2):
        copies.append(
            pltpu.make_async_remote_copy(
                src_ref=part.at[zt, yh * 2 + 1 - me.co],
                dst_ref=core_recv.at[zt, yh],
                send_sem=send_sem.at[i, yh],
                recv_sem=recv_sem.at[i, yh],
                device_id=me.at(co=1 - me.co),
                device_id_type=MESH,
            )
        )
    return copies


class Pair:
    def __init__(self, copies):
        self.copies = copies

    def wait_recv(self):
        for copy in self.copies:
            copy.wait_recv()


def core_copies_of(me, part, core_recv, send_sem, recv_sem):
    return [
        Pair(core_copy(me, part, core_recv, send_sem, recv_sem, me.dz(z_order(i) - 8), i))
        for i in range(8)
    ]


def weight_partial(me, rows_ref, right, part, core_recv, send_sem, recv_sem):
    def body(i, carry):
        zt = (me.z + z_order(i)) % 8
        at = pl.ds(pl.multiple_of(zt * 384, 128), 384)
        left = rows_ref[:, :, at].reshape(1024, 384)
        result = dot(left, right(), TN).astype(BF16)
        part[zt] = result.reshape(4, 96, result.shape[-1])
        for copy in core_copy(me, part, core_recv, send_sem, recv_sem, zt, i):
            copy.start()
        return carry

    lax.fori_loop(0, 8, body, 0)


def attention_rows(q, k, v, g, mask):
    factor = 128**-0.5
    s = dot(q, k, NT) * factor
    if mask is not None:
        s = jnp.where(mask, s, -1e30)
    e = jnp.exp(s - jnp.max(s, axis=-1, keepdims=True))
    p = e * (1.0 / jnp.sum(e, axis=-1, keepdims=True))
    dp = dot(g, v, NT)
    inner = jnp.sum(p * dp, axis=-1, keepdims=True)
    ds = (p * (dp - inner) * factor).astype(BF16)
    return dot(ds, k), dot(ds, q, TN), dot(p.astype(BF16), g, TN)


def temporal(h, piece, qkv, grad, dk, dv, out):
    tile = 128
    rows = lax.broadcasted_iota(jnp.int32, (tile, 1024), 0)
    cols = lax.broadcasted_iota(jnp.int32, (tile, 1024), 1)
    mask = (rows % 16) == (cols % 16)

    def body(t, carry):
        at = pl.ds(pl.multiple_of(t * tile, tile), tile)
        one, two, three = attention_rows(
            qkv[0, h, at, :], qkv[1, h], qkv[2, h], grad[h, at, :], mask
        )
        out[at, pl.ds(h * 384, 128)] = one.astype(BF16)
        dk[...] += two
        dv[...] += three
        return carry

    if piece == 0:
        dk[...] = jnp.zeros_like(dk)
        dv[...] = jnp.zeros_like(dv)
    lax.fori_loop(piece * 4, piece * 4 + 4, body, 0)
    if piece == 0:
        return
    out[:, pl.ds(h * 384 + 128, 128)] = dk[...].astype(BF16)
    out[:, pl.ds(h * 384 + 256, 128)] = dv[...].astype(BF16)


def unit_of(y):
    values = y.astype(F32)
    center = values - jnp.mean(values, axis=-1, keepdims=True)
    inverse = lax.rsqrt(jnp.mean(center * center, axis=-1, keepdims=True) + 1e-06)
    return center * inverse, inverse


def main_kernel(
    w_ref, v_ref, y_ref, res_ref, shift_ref, scale_ref, qkv_ref, grad_ref, sout_ref, sqkv_ref,
    out_ref, ig_ref, wt_ref, ws_ref,
    wf, nf, dq, dk, dv, part, from_y, quarter, half, last_y,
    wpart, core_recv, ring, across, igf,
    gso, byf, gout, wspart, core_recv_s, from_yh, from_z,
    send_sem, recv_sem, core_send, core_recv_sem, core_send_s, core_recv_sem_s,
    gso_send, gso_recv, out_send, out_recv,
    qkv, grad, res, sout, sqkv, local_sem,
):
    me = Place()
    net = Net(send_sem, recv_sem)
    s_own = me.yl * 4 + me.x
    p_own = lax.axis_index("pos")
    far = 1 - me.yl
    local_copies = [
        pltpu.make_async_copy(source, target, local_sem.at[i])
        for i, (source, target) in enumerate(
            [(qkv_ref, qkv), (grad_ref, grad), (res_ref, res), (sout_ref, sout), (sqkv_ref, sqkv)]
        )
    ]
    for copy in local_copies:
        copy.start()
    meet(me.neighbours(True, True))

    def norm_tile(i, carry):
        at = pl.ds(pl.multiple_of(i * 16, 16), 16)
        unit, _ = unit_of(y_ref[at, :])
        nf[s_own, at, :] = (unit * (1.0 + scale_ref[...]) + shift_ref[...]).astype(BF16)
        return carry

    for h in range(2):
        for c in range(3):
            wf[p_own, :, pl.ds((h * 3 + c) * 128, 128)] = w_ref[h, c]
        wf[p_own, :, pl.ds(768 + h * 128, 128)] = v_ref[h]
    first = gather_pos(net, me, wf)
    second = gather_seq(net, me, nf, lambda at: None)
    next(first)
    lax.fori_loop(0, 8, norm_tile, 0)
    next(second)
    for copy in local_copies[:2]:
        copy.wait()
    temporal(0, 0, qkv, grad, dk, dv, dq)
    next(first)
    next(first)
    next(second)
    temporal(0, 1, qkv, grad, dk, dv, dq)
    next(second)
    next(first)
    temporal(1, 0, qkv, grad, dk, dv, dq)
    next(first)
    next(second)
    temporal(1, 1, qkv, grad, dk, dv, dq)
    next(first)
    next(second)
    next(first)
    next(first)
    next(second)
    for _ in first:
        pass

    def partial(x):
        lhs = jnp.concatenate(
            [dq[pl.ds(pl.multiple_of((yl * 4 + x) * 128, 128), 128), :] for yl in range(2)], axis=0
        )

        def body(z, carry):
            w = wf[pl.ds(z * 4, 4), :, pl.ds(0, 768)].reshape(384, 768)
            result = dot(lhs, w, NT).astype(BF16)
            at = pl.ds(pl.multiple_of(z * 384, 128), 384)
            part[x, :, at] = result[:128]
            part[4 + x, :, at] = result[128:]
            return carry

        lax.fori_loop(0, 8, body, 0)

    def low(yl):
        return lambda x: part.at[yl * 4 + x, :, pl.ds(0, CUT)]

    def high(x):
        return part.at[me.yl * 4 + x, :, pl.ds(CUT, REST)]

    def to_partner(x):
        return net.send(part.at[far * 4 + x, :, pl.ds(CUT, REST)], from_y.at[x], me.at(yl=far))

    def take(i):
        swaps[i].wait_recv()
        add_into(high(order[i]), [from_y.at[order[i]]], 128)

    swaps = {}
    order = [me.dx(2), me.dx(1), me.dx(-1), me.x]
    red_far = reduce_x(net, me, low(far), CUT, quarter.at[0], half.at[0])
    red_own = reduce_x(net, me, low(me.yl), CUT, quarter.at[1], half.at[1])
    red_two = reduce_x(net, me, high, REST, quarter.at[2], half.at[2])
    partial(order[0])
    next(red_far)
    swaps[0] = to_partner(order[0])
    next(red_own)
    for i in range(1, 4):
        partial(order[i])
        swaps[i] = to_partner(order[i])
    next(red_far)
    take(0)
    next(red_two)
    next(red_own)

    for _ in second:
        pass
    weight_partial(me, nf, lambda: dq[...], wpart, core_recv, core_send, core_recv_sem)
    core = core_copies_of(me, wpart, core_recv, core_send, core_recv_sem)

    def wt_total(value):
        for h in range(2):
            for c in range(3):
                wt_ref[h, c] = value[:, (h * 3 + c) * 128 : (h * 3 + c + 1) * 128]

    def ws_total(value):
        for h in range(2):
            ws_ref[h] = value[:, h * 128 : (h + 1) * 128]

    wt_steps = reduce_pos_ring(net, me, wpart, core_recv, core, ring, across, wt_total)

    take(1)
    take(2)
    next(wt_steps)
    for _ in red_far:
        pass
    swap = net.send(part.at[far * 4 + me.x, :, pl.ds(0, CUT)], last_y, me.at(yl=far))
    next(red_two)
    next(wt_steps)
    take(3)
    for _ in red_own:
        pass
    for _ in red_two:
        pass
    swap.wait_recv()

    for copy in local_copies[2:]:
        copy.wait()

    def back_tile(i, carry):
        at = pl.ds(pl.multiple_of(i * 16, 16), 16)
        total = part[s_own, at, :].astype(F32)
        more = total[:, :CUT] + last_y[at, :].astype(F32)
        total = jnp.concatenate([more, total[:, CUT:]], axis=1)
        unit, inverse = unit_of(y_ref[at, :])
        scaled = total * (1.0 + scale_ref[...])
        one = jnp.mean(scaled, axis=-1, keepdims=True)
        two = jnp.mean(scaled * unit, axis=-1, keepdims=True)
        result = res[at, :].astype(F32) + inverse * (scaled - one - unit * two)
        result = result.astype(BF16)
        igf[s_own, at, :] = result
        ig_ref[at, :] = result
        return carry

    lax.fori_loop(0, 8, back_tile, 0)

    def gso_copy(p_to, p_from):
        return pltpu.make_async_remote_copy(
            src_ref=gso.at[p_to],
            dst_ref=byf.at[p_from],
            send_sem=gso_send.at[p_to],
            recv_sem=gso_recv.at[p_from],
            device_id=(s_own, p_to),
            device_id_type=MESH,
        )

    def project(blocks):
        def body(i, carry):
            s = blocks[0]
            for n in range(1, len(blocks)):
                s = jnp.where(i == n, blocks[n], s)
            w = wf[:, :, pl.ds(768, 256)].reshape(3072, 256)
            result = dot(igf[s], w).astype(BF16).reshape(4, 32, 256)
            gso[pl.ds(s * 4, 4)] = result
            for n in range(4):
                p_to = s * 4 + n

                @pl.when(p_to == p_own)
                def _():
                    byf[p_to] = result[n]

                @pl.when(p_to != p_own)
                def _():
                    gso_copy(p_to, p_own).start()

            return carry

        lax.fori_loop(0, len(blocks), body, 0)

    def others(body):
        def step(i, carry):
            body((p_own + 16 + (1 - 2 * (i % 2)) * ((i + 1) // 2)) % 32)
            return carry

        lax.fori_loop(0, 31, step, 0)

    def out_copy(h, p_to, p_from):
        return pltpu.make_async_remote_copy(
            src_ref=gout.at[p_to, h],
            dst_ref=out_ref.at[:, h, p_from],
            send_sem=out_send.at[h, p_to],
            recv_sem=out_recv.at[h, p_from],
            device_id=(s_own, p_to),
            device_id_type=MESH,
        )

    def attend(h):
        if h == 0:
            others(lambda p: gso_copy(p_own, p).wait_recv())
        spatial(h, sqkv, byf, dk, dv, gout)
        out_ref[:, h, p_own] = gout[p_own, h]
        others(lambda p: out_copy(h, p, p_own).start())

    pending = []

    def come():
        blocks = list(pending)
        pending.clear()
        project(blocks)
        return blocks

    last = gather_seq(net, me, igf, lambda at: pending.append(at[0] * 4 + at[1]))
    next(last)
    come()
    next(wt_steps)
    next(last)
    next(last)
    next(last)
    come()
    next(last)
    next(wt_steps)
    next(last)
    come()
    next(last)
    come()
    for _ in last:
        pass
    come()
    for _ in wt_steps:
        pass

    weight_partial(
        me,
        igf,
        lambda: jnp.concatenate([sout[0], sout[1]], axis=1),
        wspart,
        core_recv_s,
        core_send_s,
        core_recv_sem_s,
    )
    core_s = core_copies_of(me, wspart, core_recv_s, core_send_s, core_recv_sem_s)
    ws_steps = reduce_pos_direct(
        net, me, wspart, core_recv_s, core_s, from_yh, from_z, ws_total
    )
    next(ws_steps)
    for h in range(2):
        attend(h)
        next(ws_steps, None)
    for _ in ws_steps:
        pass
    for h in range(2):
        others(lambda p: out_copy(h, p_own, p).wait_recv())
    for h in range(2):
        others(lambda p: out_copy(h, p, p_own).wait_send())
    others(lambda p: gso_copy(p, p_own).wait_send())
    for pair in core + core_s:
        for copy in pair.copies:
            copy.wait_send()
    net.finish()


def spatial(h, qkv, byf, dk, dv, gout):
    tile = 256

    def frame(f, carry):
        def rows(t, inner):
            at = pl.ds(pl.multiple_of(t * tile, tile), tile)
            blocks = pl.ds(t * (tile // 16), tile // 16)
            g = byf[blocks, pl.ds(f * 16, 16), pl.ds(h * 128, 128)].reshape(tile, 128)
            one, two, three = attention_rows(
                qkv[0, h, f, at, :], qkv[1, h, f], qkv[2, h, f], g, None
            )
            gout[blocks, h, 0, f] = one.astype(BF16).reshape(tile // 16, 16, 128)
            dk[:512] += two
            dv[:512] += three
            return inner

        dk[:512] = jnp.zeros((512, 128), F32)
        dv[:512] = jnp.zeros((512, 128), F32)
        lax.fori_loop(0, 512 // tile, rows, 0)
        gout[:, h, 1, f] = dk[:512].astype(BF16).reshape(32, 16, 128)
        gout[:, h, 2, f] = dv[:512].astype(BF16).reshape(32, 16, 128)
        return carry

    lax.fori_loop(0, 2, frame, 0)


def vmem():
    return pl.BlockSpec(memory_space=pltpu.VMEM)


def anywhere():
    return pl.BlockSpec(memory_space=pl.ANY)


def ring_scratch(width):
    return [
        pltpu.VMEM((8, 2, 96, width), BF16),
        pltpu.VMEM((2, 4, 2, 96, width), BF16),
        pltpu.VMEM((96, width), BF16),
    ]


def run_main(w, v, y, res, shift, scale, qkv, grad, sout, sqkv):
    dma = pltpu.SemaphoreType.DMA
    return pl.pallas_call(
        main_kernel,
        out_shape=(
            jax.ShapeDtypeStruct((3, 2, 32, 2, 16, 128), BF16),
            jax.ShapeDtypeStruct((128, 3072), BF16),
            jax.ShapeDtypeStruct((2, 3, 96, 128), F32),
            jax.ShapeDtypeStruct((2, 96, 128), F32),
        ),
        in_specs=[vmem(), vmem(), vmem(), anywhere(), vmem(), vmem()] + [anywhere()] * 4,
        out_specs=(vmem(),) * 4,
        scratch_shapes=[
            pltpu.VMEM((32, 96, 1024), BF16),
            pltpu.VMEM((8, 128, 3072), BF16),
            pltpu.VMEM((1024, 768), BF16),
            pltpu.VMEM((1024, 128), F32),
            pltpu.VMEM((1024, 128), F32),
            pltpu.VMEM((8, 128, 3072), BF16),
            pltpu.VMEM((4, 128, REST), BF16),
            pltpu.VMEM((3, 2, 128, CUT // 2), BF16),
            pltpu.VMEM((3, 2, 128, CUT), BF16),
            pltpu.VMEM((128, CUT), BF16),
            pltpu.VMEM((8, 4, 96, 768), BF16),
            *ring_scratch(768),
            pltpu.VMEM((8, 128, 3072), BF16),
            pltpu.VMEM((32, 32, 256), BF16),
            pltpu.VMEM((32, 32, 256), BF16),
            pltpu.VMEM((32, 2, 3, 2, 16, 128), BF16),
            pltpu.VMEM((8, 4, 96, 256), BF16),
            pltpu.VMEM((8, 2, 96, 256), BF16),
            pltpu.VMEM((8, 96, 256), BF16),
            pltpu.VMEM((8, 96, 256), BF16),
            dma((130,)),
            dma((130,)),
            dma((8, 2)),
            dma((8, 2)),
            dma((8, 2)),
            dma((8, 2)),
            dma((32,)),
            dma((32,)),
            dma((2, 32)),
            dma((2, 32)),
            pltpu.VMEM((3, 2, 1024, 128), BF16),
            pltpu.VMEM((2, 1024, 128), BF16),
            pltpu.VMEM((128, 3072), BF16),
            pltpu.VMEM((2, 1024, 128), BF16),
            pltpu.VMEM((3, 2, 2, 512, 128), BF16),
            dma((5,)),
        ],
        compiler_params=pltpu.CompilerParams(
            collective_id=0, has_side_effects=True, vmem_limit_bytes=63 << 20
        ),
        name="main",
    )(w, v, y, res, shift, scale, qkv, grad, sout, sqkv)


def local(
    y_rows, grad_res, shift, scale_mod, temporal_qkv, temporal_grad,
    spatial_qkv, spatial_out, w_temporal, w_spatial,
):
    grads, ig, wt, ws = run_main(
        jnp.transpose(w_temporal, (0, 2, 1, 3)),
        w_spatial,
        y_rows.reshape(128, 3072),
        grad_res.reshape(128, 3072),
        shift.reshape(1, 3072),
        scale_mod.reshape(1, 3072),
        temporal_qkv.reshape(3, 2, 1024, 128),
        temporal_grad.reshape(2, 1024, 128),
        spatial_out.reshape(2, 1024, 128),
        spatial_qkv,
    )
    by_heads = grads.reshape(3, 2, 64, 16, 128)
    wt = jnp.transpose(wt, (0, 2, 1, 3))
    return by_heads, ig.reshape(8, 16, 3072), wt, ws


def solution(mesh):
    placed = (
        P("seq", "pos", None),
        P("seq", "pos", None),
        P(),
        P(),
        P(None, "seq", None, "pos", None),
        P("seq", None, "pos", None),
        P(None, "seq", "pos", None, None),
        P("seq", None, "pos", None),
        P("seq", "pos", None, None),
        P("seq", "pos", None),
    )
    return jax.shard_map(
        local,
        mesh=mesh,
        in_specs=placed,
        out_specs=(
            P(None, "seq", None, "pos", None),
            P("seq", "pos", None),
            P("seq", "pos", None, None),
            P("seq", "pos", None),
        ),
        check_vma=False,
    )
```
